128 devices in a mesh: shard: 64 (over z, y, x), basis: 2 (over core).
Axes of the slice: x: 4, y: 4, z: 4, core: 2. Of those that a mesh axis runs over, the one named last changes fastest.
Arguments:
- features: bfloat16 [393216, 1024], P('shard', 'basis'), may hold values from -6 to 6
- bases: bfloat16 [2, 1024, 1024], P('basis'), may hold values from -0.1875 to 0.1875
- coeffs: float32 [14824, 2], replicated, may hold values from -3 to 3
- block_lists: int32 [64, 64, 1], P('shard'), may hold values from 0 to 47
- block_counts: int32 [64, 64], P('shard'), may hold values from 0 to 1, as said below
- tile_rel: int32 [64, 52], P('shard'), may hold values from 0 to 14823
- dest_ids: int32 [64, 3328], P('shard'), may hold values from 0 to 127
Outputs:
- aggregated: bfloat16 [16384, 1024], P(('shard', 'basis'))
The draws below stay inside these ranges and needn't reach their ends.
Inputs may be any that keep to these rules, and one draw needn't show every extreme that they name: `block_counts`: each row g sums to exactly 26; one owner, the same in every row, has count 1 in every row. `block_lists`: slots at or beyond the count hold valid block numbers that are not used.
All inputs are finite; a program needn't handle non-finite values.
Results may differ from the reference program's by a relative error of at most 0.0049.
Values may be sent and summed in bfloat16 or wider, within the bound.
No kernel may reach another device: no remote copies, remote signals or barrier semaphores. Data moves between devices by JAX's collectives and lax.ppermute only.
A program may use at most 128 MiB of HBM per device.

```python
import math
import jax
import jax.numpy as jnp
import numpy as np
from jax import lax

D = 1024
RELS = 14824
BROWS = 128
TILE = 64
BLK_GRP = 26
OWN_BLK = 48
DST_DEV = 128
CAP = 1
BASES = 2
ROWS_DEV = 1664
TILES_GRP = 52
DST_GRP = 256
ENTITIES = 393216
N_SHARD = 64


def draw_block_counts(key, part):
    key = jax.random.fold_in(key, 11)
    key_hot, key_double, key_order = jax.random.split(key, 3)
    remain = BLK_GRP - CAP
    least_double = max(0, -(-(remain - (N_SHARD - 1)) // max(CAP - 1, 1)))
    most_double = remain // CAP
    hot_owner = jax.random.randint(key_hot, (), 0, N_SHARD)
    doubled = jax.random.randint(key_double, (N_SHARD, 1), least_double, most_double + 1)
    owner_ids = jnp.arange(N_SHARD, dtype=jnp.int32)
    shuffle_score = jax.random.randint(key_order, (N_SHARD, N_SHARD), 0, 1 << 20) * N_SHARD + owner_ids[None, :]
    shuffle_score = jnp.where(owner_ids[None, :] == hot_owner, -1, shuffle_score)
    owner_rank = jnp.argsort(jnp.argsort(shuffle_score, axis=1), axis=1)
    singles_end = doubled + remain - doubled * CAP
    full_slot = (owner_rank == 0) | (owner_rank <= doubled)
    single_slot = (owner_rank > doubled) & (owner_rank <= singles_end)
    return jnp.where(full_slot, CAP, jnp.where(single_slot, 1, 0)).astype(jnp.int32)


def plant(values, key, smallest, high):
    place = [jax.random.randint(jax.random.fold_in(key, axis), (), 0, length) for axis, length in enumerate(values.shape)]
    widest = values.shape.index(max(values.shape))
    beside = place[:widest] + [(place[widest] + 1) % values.shape[widest]] + place[widest + 1:]
    return values.at[tuple(place)].set(smallest).at[tuple(beside)].set(high)


def shard_levels(stream_key, extent, pieces, smallest, high):
    factor_of = 1.0
    for dim, parts in pieces:
        steps = jax.random.uniform(jax.random.fold_in(jax.random.fold_in(stream_key, 6), dim), (parts,), jnp.float32, smallest / len(pieces), high / len(pieces))
        factor_of = factor_of * jnp.repeat(jnp.exp(steps), extent[dim] // parts).reshape((-1,) + (1,) * (len(extent) - 1 - dim))
    return factor_of


def rank_table(count, skew):
    weights = [(1 << 20) // math.isqrt(standing ** skew) + 1 for standing in range(1, count + 1)]
    width = 1 + sum(weights) // (1 << 30)
    return np.cumsum(np.array([max(1, weight // width) for weight in weights]))


def skewed_ids(key, dims, amount, lean):
    table = rank_table(amount, lean)
    ticket = jax.random.randint(jax.random.fold_in(key, 1), dims, 0, int(table[amount - 1]))
    grade = jnp.searchsorted(jnp.asarray(table, jnp.int32), ticket, side="right")
    return jax.random.permutation(jax.random.fold_in(key, 2), amount)[grade].astype(jnp.int32)


def scatter_about(key, shape, width, most, cuts=(), kind=jnp.bfloat16):
    array = jax.random.normal(key, shape, jnp.float32) * width
    if len(cuts) > 0:
        array = shard_levels(key, shape, cuts, -0.22, 0.18) * array
    return jnp.clip(array, min=-most, max=most).astype(kind)


def setup_inputs(seed: int = 0) -> dict:
    streams_of = jax.random.split(jax.random.key(seed), 8)
    return {
        "features": scatter_about(streams_of[0], (ENTITIES, D), 1.0, 6.0, ((0, 64), (1, 2))),
        "bases": scatter_about(streams_of[1], (BASES, D, D), D ** -0.5, 0.1875, ((0, 2),)),
        "coeffs": scatter_about(streams_of[2], (RELS, BASES), 0.5, 3.0, (), jnp.float32),
        "block_lists": plant(jax.random.randint(streams_of[3], (N_SHARD, N_SHARD, CAP), 0, OWN_BLK), jax.random.fold_in(streams_of[3], 1), 0, OWN_BLK - 1).astype(jnp.int32),
        "block_counts": draw_block_counts(jax.random.fold_in(streams_of[7], 71), 0),
        "tile_rel": plant(skewed_ids(streams_of[5], (N_SHARD, TILES_GRP), RELS, 2), jax.random.fold_in(streams_of[5], 3), 0, RELS - 1).astype(jnp.int32),
        "dest_ids": plant(jax.random.randint(streams_of[6], (N_SHARD, BLK_GRP * BROWS), 0, DST_DEV), jax.random.fold_in(streams_of[6], 1), 0, DST_DEV - 1).astype(jnp.int32),
    }


def select_slots(count_row, block_total, slot_cap):
    slot_ids = jnp.arange(count_row.shape[0] * slot_cap, dtype=jnp.int32)
    live_slot = (slot_ids % slot_cap) < count_row[slot_ids // slot_cap]
    position = jnp.cumsum(live_slot.astype(jnp.int32)) - 1
    wanted_pos = jnp.arange(block_total, dtype=jnp.int32)
    match_hit = live_slot[None, :] & (position[None, :] == wanted_pos[:, None])
    return jnp.sum(jnp.where(match_hit, slot_ids[None, :], 0), axis=1).astype(jnp.int32)


def reference(features, bases, coeffs, block_lists, block_counts, tile_rel, dest_ids):
    blocks_all = features.reshape(N_SHARD * OWN_BLK, BROWS, D)
    rows_dev = ROWS_DEV
    group_size = BLK_GRP * BROWS

    def one_group(group_args):
        group_lists, group_counts, group_rels, group_dests = group_args
        chosen = select_slots(group_counts, BLK_GRP, CAP)
        owner_idx = (chosen // CAP).astype(jnp.int32)
        slot_idx = (chosen % CAP).astype(jnp.int32)
        block_ids = (owner_idx * OWN_BLK + group_lists[owner_idx, slot_idx]).astype(jnp.int32)
        group_rows = blocks_all[block_ids].reshape(group_size, D)
        row_coef = jnp.repeat(coeffs[group_rels], TILE, axis=0)

        def add_basis(running, basis_idx):
            proj = jnp.dot(group_rows, bases[basis_idx], preferred_element_type=jnp.float32).astype(jnp.bfloat16)
            weight = lax.dynamic_index_in_dim(row_coef, basis_idx, 1, keepdims=True)
            return running + weight * proj.astype(jnp.float32), None

        messages, _ = lax.scan(add_basis, jnp.zeros((group_size, D), jnp.float32), jnp.arange(BASES, dtype=jnp.int32))
        target = (jnp.arange(group_size, dtype=jnp.int32) // rows_dev) * DST_DEV + group_dests
        summed = jax.ops.segment_sum(messages, target, num_segments=DST_GRP)
        indegree = jax.ops.segment_sum(jnp.ones((group_size,), jnp.float32), target, num_segments=DST_GRP)
        return (summed / jnp.maximum(indegree, 1.0)[:, None]).astype(jnp.bfloat16)

    result_rows = lax.map(one_group, (block_lists, block_counts, tile_rel, dest_ids))
    return result_rows.reshape(N_SHARD * DST_GRP, D)
```

```python
import functools

import jax
import jax.numpy as jnp
from jax import lax
from jax.experimental import pallas as pl
from jax.experimental.pallas import tpu as pltpu
from jax.sharding import PartitionSpec as P

BROWS = 128
TILE = 64
DST = 128
SIDE = 4
CHIPS = SIDE**3
AXES = ("shard", "basis")
HOP2 = (2, 1, 3, 0)
BF16 = jnp.bfloat16
F32 = jnp.float32
VMEM_LIMIT = 48 * 1024 * 1024


def device_id(x, y, z, core):
    return ((z % SIDE * SIDE + y % SIDE) * SIDE + x % SIDE) * 2 + core


def pairs(target):
    found = []
    for z in range(SIDE):
        for y in range(SIDE):
            for x in range(SIDE):
                for core in range(2):
                    found.append((device_id(x, y, z, core), device_id(*target(x, y, z, core))))
    assert len({to for _, to in found}) == len(found)
    return found


def hop1_pairs(step, crossed):
    def target(x, y, z, core):
        kind = 1 - core if crossed else core
        return (x + step, y, z, 0) if kind == 0 else (x, y + step, z, 1)

    return pairs(target)


def hop2_pairs(step):
    return pairs(lambda x, y, z, core: (x, y, z + step, core))


MATCHED = ((0, 0), (2, 1), (2, 0), (0, 1))
UNMATCHED = ((1, 1), (1, 0), (3, 1), (3, 0))


def hop3_pairs(send):
    def target(x, y, z, core):
        step, half = (MATCHED if (x + y + z) % 2 == core else UNMATCHED)[send]
        return (x, y + step, z, half) if core == 0 else (x + step, y, z, half)

    return pairs(target)


def coordinates():
    chip = lax.axis_index("shard")
    return chip % SIDE, chip // SIDE % SIDE, chip // (SIDE * SIDE), lax.axis_index("basis")


def group_of(x, y, z, kind, which):
    y_end = 2 * which + (x + z) % 2
    x_end = 2 * which + (y + z + 1) % 2
    return jnp.where(kind == 0, (z * SIDE + y_end) * SIDE + x, (z * SIDE + y) * SIDE + x_end)


def notes_kernel(kind_ref, counts_ref, dests_ref, rels_ref, lists_ref, out_ref):
    rows = CHIPS * 8
    blocks = dests_ref.shape[0]
    counts = counts_ref[...]
    before = (
        lax.broadcasted_iota(jnp.int32, (CHIPS, CHIPS), 0)
        < lax.broadcasted_iota(jnp.int32, (CHIPS, CHIPS), 1)
    ).astype(F32)
    used = counts.astype(F32)
    rank = jnp.dot(jnp.broadcast_to(used, (8, CHIPS)), before, preferred_element_type=F32)[:1]
    where = jnp.where(counts > 0, rank, -1.0)
    row = lax.broadcasted_iota(jnp.int32, (rows, 1), 0)
    slot, place = row // 8, row % 8
    line = place % SIDE
    owner = jnp.where(
        kind_ref[0] == 0, slot // SIDE * SIDE + line, slot // 16 * 16 + line * SIDE + slot % SIDE
    )
    lane = lax.broadcasted_iota(jnp.int32, (rows, CHIPS), 1)
    position = jnp.sum(jnp.where(lane == owner, where, 0.0), axis=1, keepdims=True)
    hit = position == lax.broadcasted_iota(jnp.int32, (rows, blocks), 1).astype(F32)
    hit = hit.astype(BF16)
    dests = jnp.dot(hit, dests_ref[...].astype(BF16), preferred_element_type=F32)
    rels = jnp.dot(hit, rels_ref[...].astype(BF16), preferred_element_type=F32)
    codes = jnp.where(position < 0, -1.0, dests + jnp.where(position >= blocks // 2, float(DST), 0.0))
    wanted = jnp.where(counts > 0, lists_ref[...], -1).astype(F32)
    block = jnp.sum(jnp.where(lane == slot, wanted, 0.0), axis=1, keepdims=True)
    other = jnp.where(lax.broadcasted_iota(jnp.int32, (rows, DST), 1) == 4, block, rels)
    out_ref[...] = jnp.where(place < SIDE, codes, other).astype(jnp.int32)


def make_notes(kind, counts, dests, rels, lists):
    blocks = dests.shape[0]
    halves = jnp.concatenate([rels // DST, rels % DST], axis=1)
    halves = jnp.pad(halves, ((0, 0), (0, DST - halves.shape[1])))
    vmem = pl.BlockSpec(memory_space=pltpu.VMEM)
    return pl.pallas_call(
        notes_kernel,
        out_shape=jax.ShapeDtypeStruct((CHIPS * 8, DST), jnp.int32),
        in_specs=[pl.BlockSpec(memory_space=pltpu.SMEM)] + [vmem] * 4,
        out_specs=vmem,
        name="notes",
    )(kind.reshape(1), counts.reshape(1, CHIPS), dests, halves, lists.reshape(1, CHIPS)).reshape(CHIPS, 8, DST)


SENDS = ((1, False), (3, False), (1, True), (3, True), (2, False), (2, True), (0, True))


def pick_kernel(step_z, wanted_ref, table_ref, *rest):
    outs, sems = rest[:-1], rest[-1]
    x, y, z, core = coordinates()
    copies = []
    for send, (step, crossed) in enumerate(SENDS):
        kind = 1 - core if crossed else core
        x_to = jnp.where(kind == 0, (x + step) % SIDE, x)
        y_to = jnp.where(kind == 0, y, (y + step) % SIDE)
        for which in range(2):
            block = wanted_ref[group_of(x_to, y_to, (z + step_z) % SIDE, kind, which)]
            start = pl.multiple_of(jnp.maximum(block, 0) * BROWS, BROWS)
            copies.append(
                (
                    block >= 0,
                    pltpu.make_async_copy(
                        table_ref.at[pl.ds(start, BROWS)], outs[send].at[which], sems.at[send, which]
                    ),
                )
            )
    for live, copy in copies:
        pl.when(live)(copy.start)
    for live, copy in copies:
        pl.when(live)(copy.wait)


def pick(step_z, wanted, table):
    width = table.shape[1]
    anywhere = pl.BlockSpec(memory_space=pl.ANY)
    return pl.pallas_call(
        functools.partial(pick_kernel, step_z),
        out_shape=[jax.ShapeDtypeStruct((2, BROWS, width), BF16)] * len(SENDS),
        in_specs=[pl.BlockSpec(memory_space=pltpu.SMEM), anywhere],
        out_specs=[anywhere] * len(SENDS),
        scratch_shapes=[pltpu.SemaphoreType.DMA((len(SENDS), 2))],
        cost_estimate=pl.CostEstimate(
            flops=0, bytes_accessed=4 * len(SENDS) * 2 * BROWS * width, transcendentals=0
        ),
        name="pick",
    )(wanted, table)


def project_kernel(step_z, codes_ref, wanted_ref, coef_ref, notes_ref, table_ref, *rest):
    received = rest[: len(SENDS)]
    own_basis, other_basis, out_ref, rows, notes, total, basis, sems, more_sems = rest[len(SENDS) :]
    x, y, z, core = coordinates()
    width = table_ref.shape[1]
    along = jnp.where(core == 0, x, y)
    lookup = {sent: received[i] for i, sent in enumerate(SENDS)}
    loads = [
        pltpu.make_async_copy(own_basis, basis.at[0], more_sems.at[0]),
        pltpu.make_async_copy(other_basis, basis.at[1], more_sems.at[1]),
    ]
    pieces, note_loads = [], []
    for which in range(2):
        group = group_of(x, y, (z + step_z) % SIDE, core, which)
        note_loads.append(pltpu.make_async_copy(notes_ref.at[group], notes.at[which], more_sems.at[2 + which]))
        note_loads[-1].start()
        for step in range(SIDE):
            line = (along - step) % SIDE
            code = codes_ref[group * SIDE + line]
            copies = []
            for part, crossed in enumerate((False, True)):
                if step == 0 and not crossed:
                    start = pl.multiple_of(jnp.maximum(wanted_ref[group], 0) * BROWS, BROWS)
                    source = table_ref.at[pl.ds(start, BROWS)]
                else:
                    source = lookup[(step, crossed)].at[which]
                copies.append(
                    pltpu.make_async_copy(source, rows.at[which, step, part], sems.at[which, step, part])
                )
            pl.when(code >= 0)(lambda copies=copies: [c.start() for c in copies] and None)
            pieces.append((which, step, line, code, copies))
    for load in loads:
        load.start()
    total[...] = jnp.zeros_like(total)
    for load in note_loads:
        load.wait()
    first_tile = lax.broadcasted_iota(jnp.int32, (1, BROWS), 1) < TILE
    dest = lax.broadcasted_iota(jnp.int32, (DST, BROWS), 0)
    for which, step, line, code, copies in pieces:

        @pl.when(code >= 0)
        def _(which=which, step=step, line=line, code=code, copies=copies):
            half = jnp.where(code >= DST, 1, 0)
            hit = notes[which, pl.ds(line, 1), :] - half * DST == dest
            chosen = []
            at = ((which * SIDE + step) * (BROWS // TILE)) * 2
            for k in range(2):
                weight = jnp.where(first_tile, coef_ref[at + k], coef_ref[at + 2 + k])
                high = weight.astype(BF16).astype(F32)
                high, low = jnp.where(hit, high, 0.0), jnp.where(hit, weight - high, 0.0)
                chosen.append(jnp.concatenate([high, low], axis=1))
            chosen = jnp.concatenate(chosen, axis=0).astype(BF16)
            for part in range(2):
                copies[part].wait()
                block = rows[which, step, part]
                added = jnp.dot(
                    chosen, jnp.concatenate([block, block], axis=0), preferred_element_type=F32
                )
                column = pl.multiple_of(jnp.where(core == part, 0, width), width)
                total[which, half, :, pl.ds(column, width)] += added

    for load in loads:
        load.wait()
    summed = [
        total[:, :, k * DST : (k + 1) * DST, :].reshape(4 * DST, 2 * width).astype(BF16) for k in range(2)
    ]
    wide = basis.shape[2]
    tile = 256
    for start in range(0, wide, tile):
        result = jnp.dot(summed[0], basis[0, :, start : start + tile], preferred_element_type=F32)
        result += jnp.dot(summed[1], basis[1, :, start : start + tile], preferred_element_type=F32)
        out_ref[:, :, start : start + tile] = result.reshape(4, DST, tile).astype(BF16)


def project(step_z, codes, wanted, coef, notes, table, received, own_basis, other_basis):
    width = table.shape[1]
    wide = own_basis.shape[1]
    anywhere = pl.BlockSpec(memory_space=pl.ANY)
    smem = pl.BlockSpec(memory_space=pltpu.SMEM)
    return pl.pallas_call(
        functools.partial(project_kernel, step_z),
        out_shape=jax.ShapeDtypeStruct((4, DST, wide), BF16),
        in_specs=[smem] * 3 + [anywhere] * (4 + len(SENDS)),
        out_specs=pl.BlockSpec(memory_space=pltpu.VMEM),
        scratch_shapes=[
            pltpu.VMEM((2, SIDE, 2, BROWS, width), BF16),
            pltpu.VMEM((2, 8, DST), jnp.int32),
            pltpu.VMEM((2, 2, 2 * DST, 2 * width), F32),
            pltpu.VMEM((2, 2 * width, wide), BF16),
            pltpu.SemaphoreType.DMA((2, SIDE, 2)),
            pltpu.SemaphoreType.DMA((4,)),
        ],
        cost_estimate=pl.CostEstimate(
            flops=2 * 4 * DST * 4 * width * wide, bytes_accessed=8 * 2**20, transcendentals=0
        ),
        compiler_params=pltpu.CompilerParams(vmem_limit_bytes=VMEM_LIMIT),
        name="project",
    )(codes, wanted, coef, notes, table, *received, own_basis, other_basis)


def merge_kernel(order_ref, *refs):
    ins, outs = refs[:SIDE], refs[SIDE:]
    for send in range(4):
        at = order_ref[send]
        result = ins[0][at].astype(F32)
        for other in ins[1:]:
            result += other[at].astype(F32)
        outs[send][...] = result.astype(BF16)


def merge(order, parts):
    wide = parts[0].shape[2]
    slab = 32
    return pl.pallas_call(
        merge_kernel,
        out_shape=[jax.ShapeDtypeStruct((DST, wide), BF16)] * 4,
        grid_spec=pltpu.PrefetchScalarGridSpec(
            num_scalar_prefetch=1,
            grid=(DST // slab,),
            in_specs=[pl.BlockSpec((4, slab, wide), lambda i, order: (0, i, 0))] * SIDE,
            out_specs=[pl.BlockSpec((slab, wide), lambda i, order: (i, 0))] * 4,
        ),
        compiler_params=pltpu.CompilerParams(vmem_limit_bytes=VMEM_LIMIT),
        name="merge",
    )(order, *parts)


def body(features, bases, coeffs, block_lists, block_counts, tile_rel, dest_ids):
    x, y, z, core = coordinates()
    blocks = tile_rel.shape[1] * TILE // BROWS
    other_basis = lax.ppermute(bases[0], "basis", [(0, 1), (1, 0)])

    sent = make_notes(
        (x + y + z) % 2,
        block_counts[0],
        dest_ids[0].reshape(blocks, BROWS),
        tile_rel[0].reshape(blocks, BROWS // TILE),
        block_lists[0, :, 0],
    )
    notes = lax.all_to_all(sent, "shard", split_axis=0, concat_axis=0, tiled=True)
    wanted = notes[:, SIDE, 4]
    codes = notes[:, :SIDE, 0].reshape(-1)
    along = jnp.where(core == 0, x, y)

    arrived = []
    for step_z in HOP2:
        picked = pick(step_z, wanted, features)
        arrived.append([lax.ppermute(buf, AXES, hop1_pairs(*send)) for buf, send in zip(picked, SENDS)])

    groups = jnp.stack([group_of(x, y, (z + s) % SIDE, core, w) for s in HOP2 for w in range(2)])
    lines = (along - jnp.arange(SIDE, dtype=jnp.int32)) % SIDE
    told = notes[groups[:, None], SIDE + lines[None, :], :4]
    coef = coeffs[told[..., :2] * DST + told[..., 2:]]
    coef = jnp.where(core == 0, coef, coef[..., ::-1]).reshape(len(HOP2), -1)

    parts = []
    for i, step_z in enumerate(HOP2):
        part = project(
            step_z, codes, wanted, coef[i], notes, features, arrived[i], bases[0], other_basis
        )
        parts.append(part if step_z == 0 else lax.ppermute(part, AXES, hop2_pairs(step_z)))

    last = jnp.where(core == 0, y, x)
    matched = (x + y + z) % 2 == core
    order = jnp.stack(
        [
            jnp.where(matched, (last + a) % SIDE // 2 * 2 + b, (last + c) % SIDE // 2 * 2 + d)
            for (a, b), (c, d) in zip(MATCHED, UNMATCHED)
        ]
    )
    merged = merge(order, parts)
    ends = [lax.ppermute(buf, AXES, hop3_pairs(send)) for send, buf in enumerate(merged)]
    summed = sum(end.astype(F32) for end in ends)

    rows_dev = blocks // 2 * BROWS
    my_dests = lax.dynamic_slice_in_dim(dest_ids[0], core * rows_dev, rows_dev)
    indegree = jnp.sum(
        (my_dests[None, :] == jnp.arange(DST, dtype=jnp.int32)[:, None]).astype(F32), axis=1
    )
    return (summed / jnp.maximum(indegree, 1.0)[:, None]).astype(BF16)


def solution(mesh):
    placed = (
        P("shard", "basis"),
        P("basis", None, None),
        P(),
        P("shard", None, None),
        P("shard", None),
        P("shard", None),
        P("shard", None),
    )
    return jax.shard_map(
        body, mesh=mesh, in_specs=placed, out_specs=P(("shard", "basis"), None), check_vma=False
    )
```

```python
import functools

import jax
import jax.numpy as jnp
from jax import lax
from jax.experimental import pallas as pl
from jax.experimental.pallas import tpu as pltpu
from jax.sharding import PartitionSpec as P

BROWS = 128
TILE = 64
DST = 128
SIDE = 4
CHIPS = SIDE**3
AXES = ("shard", "basis")
HOP2 = (2, 1, 3, 0)
BF16 = jnp.bfloat16
F32 = jnp.float32
VMEM_LIMIT = 48 * 1024 * 1024


def device_id(x, y, z, core):
    return ((z % SIDE * SIDE + y % SIDE) * SIDE + x % SIDE) * 2 + core


def pairs(target):
    found = []
    for z in range(SIDE):
        for y in range(SIDE):
            for x in range(SIDE):
                for core in range(2):
                    found.append((device_id(x, y, z, core), device_id(*target(x, y, z, core))))
    assert len({to for _, to in found}) == len(found)
    return found


def hop1_pairs(step, crossed):
    def target(x, y, z, core):
        kind = 1 - core if crossed else core
        return (x + step, y, z, 0) if kind == 0 else (x, y + step, z, 1)

    return pairs(target)


def hop2_pairs(step):
    return pairs(lambda x, y, z, core: (x, y, z + step, core))


MATCHED = ((0, 0), (2, 1), (2, 0), (0, 1))
UNMATCHED = ((1, 1), (1, 0), (3, 1), (3, 0))


def hop3_pairs(send):
    def target(x, y, z, core):
        step, half = (MATCHED if (x + y + z) % 2 == core else UNMATCHED)[send]
        return (x, y + step, z, half) if core == 0 else (x + step, y, z, half)

    return pairs(target)


def coordinates():
    chip = lax.axis_index("shard")
    return chip % SIDE, chip // SIDE % SIDE, chip // (SIDE * SIDE), lax.axis_index("basis")


def group_of(x, y, z, kind, which):
    y_end = 2 * which + (x + z) % 2
    x_end = 2 * which + (y + z + 1) % 2
    return jnp.where(kind == 0, (z * SIDE + y_end) * SIDE + x, (z * SIDE + y) * SIDE + x_end)


def notes_kernel(blocks, counts_ref, dests_ref, rels_ref, lists_ref, out_ref):
    rows = CHIPS * 8
    x, y, z, _ = coordinates()
    counts = counts_ref[...]
    before = (
        lax.broadcasted_iota(jnp.int32, (CHIPS, CHIPS), 0)
        < lax.broadcasted_iota(jnp.int32, (CHIPS, CHIPS), 1)
    ).astype(F32)
    used = jnp.broadcast_to(counts.astype(F32), (8, CHIPS))
    rank = jnp.dot(used, before, preferred_element_type=F32)[:1]
    where = jnp.where(counts > 0, rank, -1.0).astype(jnp.int32)
    row = lax.broadcasted_iota(jnp.int32, (rows, 1), 0)
    slot, place = row // 8, row % 8
    line = place % SIDE
    owner = jnp.where(
        (x + y + z) % 2 == 0,
        slot // SIDE * SIDE + line,
        slot // 16 * 16 + line * SIDE + slot % SIDE,
    )

    def lookup(values, index):
        lane = lax.broadcasted_iota(jnp.int32, (rows, values.shape[1]), 1)
        return jnp.sum(jnp.where(lane == index, values, 0), axis=1, keepdims=True)

    position = lookup(where, owner)
    hit = (position == lax.broadcasted_iota(jnp.int32, (rows, blocks), 1)).astype(BF16)
    dests = jnp.concatenate([dests_ref[:, p * BROWS : (p + 1) * BROWS] for p in range(blocks)], axis=0)
    dests = jnp.dot(hit, dests.astype(BF16), preferred_element_type=F32).astype(jnp.int32)
    codes = jnp.where(position < 0, -1, dests + jnp.where(position >= blocks // 2, DST, 0))
    block = lookup(jnp.where(counts > 0, lists_ref[...], -1), slot)
    lane = lax.broadcasted_iota(jnp.int32, (rows, DST), 1)
    other = block
    for tile in range(BROWS // TILE):
        rel = lookup(rels_ref[...], position * (BROWS // TILE) + tile)
        other = jnp.where(lane == tile, rel, other)
    out_ref[...] = jnp.where(place < SIDE, codes, other)


def make_notes(counts, dests, rels, lists):
    vmem = pl.BlockSpec(memory_space=pltpu.VMEM)
    return pl.pallas_call(
        functools.partial(notes_kernel, dests.shape[1] // BROWS),
        out_shape=jax.ShapeDtypeStruct((CHIPS * 8, DST), jnp.int32),
        in_specs=[vmem] * 4,
        out_specs=vmem,
        name="notes",
    )(counts, dests, rels, lists).reshape(CHIPS, 8, DST)


SENDS = ((1, False), (3, False), (1, True), (3, True), (2, False), (2, True), (0, True))


def pick_kernel(step_z, wanted_ref, table_ref, *rest):
    outs, (held, sems) = rest[: len(SENDS)], rest[len(SENDS) :]
    x, y, z, core = coordinates()
    copies = []
    for send, (step, crossed) in enumerate(SENDS):
        kind = 1 - core if crossed else core
        x_to = jnp.where(kind == 0, (x + step) % SIDE, x)
        y_to = jnp.where(kind == 0, y, (y + step) % SIDE)
        for which in range(2):
            block = wanted_ref[group_of(x_to, y_to, (z + step_z) % SIDE, kind, which)]
            start = pl.multiple_of(jnp.maximum(block, 0) * BROWS, BROWS)
            place = held.at[send, which]
            load = pltpu.make_async_copy(table_ref.at[pl.ds(start, BROWS)], place, sems.at[0, send, which])
            store = pltpu.make_async_copy(place, outs[send].at[which], sems.at[1, send, which])
            pl.when(block >= 0)(load.start)
            copies.append((block >= 0, load, store))

    def hand_on(load, store):
        load.wait()
        store.start()

    for live, load, store in copies:
        pl.when(live)(functools.partial(hand_on, load, store))
    for live, load, store in copies:
        pl.when(live)(store.wait)


def pick(step_z, wanted, table):
    width = table.shape[1]
    hbm = pl.BlockSpec(memory_space=pltpu.HBM)
    return pl.pallas_call(
        functools.partial(pick_kernel, step_z),
        out_shape=[jax.ShapeDtypeStruct((2, BROWS, width), BF16)] * len(SENDS),
        in_specs=[pl.BlockSpec(memory_space=pltpu.SMEM), hbm],
        out_specs=[hbm] * len(SENDS),
        scratch_shapes=[
            pltpu.VMEM((len(SENDS), 2, BROWS, width), BF16),
            pltpu.SemaphoreType.DMA((2, len(SENDS), 2)),
        ],
        cost_estimate=pl.CostEstimate(
            flops=0, bytes_accessed=4 * len(SENDS) * 2 * BROWS * width, transcendentals=0
        ),
        name="pick",
    )(wanted, table)


def project_kernel(step_z, codes_ref, wanted_ref, coef_ref, notes_ref, table_ref, *rest):
    received = rest[: len(SENDS)]
    own_basis, other_basis, out_ref, rows, notes, total, basis, sems, more_sems = rest[len(SENDS) :]
    x, y, z, core = coordinates()
    width = table_ref.shape[1]
    along = jnp.where(core == 0, x, y)
    lookup = {sent: received[i] for i, sent in enumerate(SENDS)}
    loads = [
        pltpu.make_async_copy(own_basis, basis.at[0], more_sems.at[0]),
        pltpu.make_async_copy(other_basis, basis.at[1], more_sems.at[1]),
    ]
    pieces, note_loads = [], []
    for which in range(2):
        group = group_of(x, y, (z + step_z) % SIDE, core, which)
        note_loads.append(pltpu.make_async_copy(notes_ref.at[group], notes.at[which], more_sems.at[2 + which]))
        note_loads[-1].start()
        for step in range(SIDE):
            line = (along - step) % SIDE
            code = codes_ref[group * SIDE + line]
            copies = []
            for part, crossed in enumerate((False, True)):
                if step == 0 and not crossed:
                    start = pl.multiple_of(jnp.maximum(wanted_ref[group], 0) * BROWS, BROWS)
                    source = table_ref.at[pl.ds(start, BROWS)]
                else:
                    source = lookup[(step, crossed)].at[which]
                copies.append(
                    pltpu.make_async_copy(source, rows.at[which, step, part], sems.at[which, step, part])
                )
            pl.when(code >= 0)(lambda copies=copies: [c.start() for c in copies] and None)
            pieces.append((which, step, line, code, copies))
    for load in loads:
        load.start()
    total[...] = jnp.zeros_like(total)
    for load in note_loads:
        load.wait()
    first_tile = lax.broadcasted_iota(jnp.int32, (1, BROWS), 1) < TILE
    dest = lax.broadcasted_iota(jnp.int32, (DST, BROWS), 0)
    for which, step, line, code, copies in pieces:

        @pl.when(code >= 0)
        def _(which=which, step=step, line=line, code=code, copies=copies):
            half = jnp.where(code >= DST, 1, 0)
            hit = notes[which, pl.ds(line, 1), :] - half * DST == dest
            chosen = []
            at = ((which * SIDE + step) * (BROWS // TILE)) * 2
            for k in range(2):
                weight = jnp.where(first_tile, coef_ref[at + k], coef_ref[at + 2 + k])
                high = weight.astype(BF16).astype(F32)
                high, low = jnp.where(hit, high, 0.0), jnp.where(hit, weight - high, 0.0)
                chosen.append(jnp.concatenate([high, low], axis=1))
            chosen = jnp.concatenate(chosen, axis=0).astype(BF16)
            for part in range(2):
                copies[part].wait()
                block = rows[which, step, part]
                added = jnp.dot(
                    chosen, jnp.concatenate([block, block], axis=0), preferred_element_type=F32
                )
                column = pl.multiple_of(jnp.where(core == part, 0, width), width)
                total[which, half, :, pl.ds(column, width)] += added

    for load in loads:
        load.wait()
    summed = [
        total[:, :, k * DST : (k + 1) * DST, :].reshape(4 * DST, 2 * width).astype(BF16) for k in range(2)
    ]
    wide = basis.shape[2]
    tile = 256
    for start in range(0, wide, tile):
        result = jnp.dot(summed[0], basis[0, :, start : start + tile], preferred_element_type=F32)
        result += jnp.dot(summed[1], basis[1, :, start : start + tile], preferred_element_type=F32)
        out_ref[:, :, start : start + tile] = result.reshape(4, DST, tile).astype(BF16)


def project(step_z, codes, wanted, coef, notes, table, received, own_basis, other_basis):
    width = table.shape[1]
    wide = own_basis.shape[1]
    hbm = pl.BlockSpec(memory_space=pltpu.HBM)
    smem = pl.BlockSpec(memory_space=pltpu.SMEM)
    return pl.pallas_call(
        functools.partial(project_kernel, step_z),
        out_shape=jax.ShapeDtypeStruct((4, DST, wide), BF16),
        in_specs=[smem] * 3 + [hbm] * (4 + len(SENDS)),
        out_specs=pl.BlockSpec(memory_space=pltpu.VMEM),
        scratch_shapes=[
            pltpu.VMEM((2, SIDE, 2, BROWS, width), BF16),
            pltpu.VMEM((2, 8, DST), jnp.int32),
            pltpu.VMEM((2, 2, 2 * DST, 2 * width), F32),
            pltpu.VMEM((2, 2 * width, wide), BF16),
            pltpu.SemaphoreType.DMA((2, SIDE, 2)),
            pltpu.SemaphoreType.DMA((4,)),
        ],
        cost_estimate=pl.CostEstimate(
            flops=2 * 4 * DST * 4 * width * wide, bytes_accessed=8 * 2**20, transcendentals=0
        ),
        compiler_params=pltpu.CompilerParams(vmem_limit_bytes=VMEM_LIMIT),
        name="project",
    )(codes, wanted, coef, notes, table, *received, own_basis, other_basis)


def merge_kernel(order_ref, *refs):
    ins, outs = refs[:SIDE], refs[SIDE:]
    for send in range(4):
        at = order_ref[send]
        result = ins[0][at].astype(F32)
        for other in ins[1:]:
            result += other[at].astype(F32)
        outs[send][...] = result.astype(BF16)


def merge(order, parts):
    wide = parts[0].shape[2]
    slab = 32
    return pl.pallas_call(
        merge_kernel,
        out_shape=[jax.ShapeDtypeStruct((DST, wide), BF16)] * 4,
        grid_spec=pltpu.PrefetchScalarGridSpec(
            num_scalar_prefetch=1,
            grid=(DST // slab,),
            in_specs=[pl.BlockSpec((4, slab, wide), lambda i, order: (0, i, 0))] * SIDE,
            out_specs=[pl.BlockSpec((slab, wide), lambda i, order: (i, 0))] * 4,
        ),
        compiler_params=pltpu.CompilerParams(vmem_limit_bytes=VMEM_LIMIT),
        name="merge",
    )(order, *parts)


def body(features, bases, coeffs, block_lists, block_counts, tile_rel, dest_ids):
    x, y, z, core = coordinates()
    blocks = tile_rel.shape[1] * TILE // BROWS
    other_basis = lax.ppermute(bases[0], "basis", [(0, 1), (1, 0)])

    sent = make_notes(block_counts, dest_ids, tile_rel, block_lists.reshape(1, CHIPS))
    notes = lax.all_to_all(sent, "shard", split_axis=0, concat_axis=0, tiled=True)
    wanted = notes[:, SIDE, 4]
    codes = notes[:, :SIDE, 0].reshape(-1)
    along = jnp.where(core == 0, x, y)

    arrived = []
    for step_z in HOP2:
        picked = pick(step_z, wanted, features)
        arrived.append([lax.ppermute(buf, AXES, hop1_pairs(*send)) for buf, send in zip(picked, SENDS)])

    groups = jnp.stack([group_of(x, y, (z + s) % SIDE, core, w) for s in HOP2 for w in range(2)])
    lines = (along - jnp.arange(SIDE, dtype=jnp.int32)) % SIDE
    told = notes[groups[:, None], SIDE + lines[None, :], : BROWS // TILE]
    coef = coeffs[told]
    coef = jnp.where(core == 0, coef, coef[..., ::-1]).reshape(len(HOP2), -1)

    parts = []
    for i, step_z in enumerate(HOP2):
        part = project(
            step_z, codes, wanted, coef[i], notes, features, arrived[i], bases[0], other_basis
        )
        parts.append(part if step_z == 0 else lax.ppermute(part, AXES, hop2_pairs(step_z)))

    last = jnp.where(core == 0, y, x)
    matched = (x + y + z) % 2 == core
    order = jnp.stack(
        [
            jnp.where(matched, (last + a) % SIDE // 2 * 2 + b, (last + c) % SIDE // 2 * 2 + d)
            for (a, b), (c, d) in zip(MATCHED, UNMATCHED)
        ]
    )
    merged = merge(order, parts)
    ends = [lax.ppermute(buf, AXES, hop3_pairs(send)) for send, buf in enumerate(merged)]
    summed = sum(end.astype(F32) for end in ends)

    rows_dev = blocks // 2 * BROWS
    my_dests = lax.dynamic_slice_in_dim(dest_ids[0], core * rows_dev, rows_dev)
    indegree = jnp.sum(
        (my_dests[None, :] == jnp.arange(DST, dtype=jnp.int32)[:, None]).astype(F32), axis=1
    )
    return (summed / jnp.maximum(indegree, 1.0)[:, None]).astype(BF16)


def solution(mesh):
    placed = (
        P("shard", "basis"),
        P("basis", None, None),
        P(),
        P("shard", None, None),
        P("shard", None),
        P("shard", None),
        P("shard", None),
    )
    return jax.shard_map(
        body, mesh=mesh, in_specs=placed, out_specs=P(("shard", "basis"), None), check_vma=False
    )
```

```python
import functools

import jax
import jax.numpy as jnp
from jax import lax
from jax.experimental import pallas as pl
from jax.experimental.pallas import tpu as pltpu
from jax.sharding import PartitionSpec as P

BROWS = 128
TILE = 64
DST = 128
SIDE = 4
CHIPS = SIDE**3
AXES = ("shard", "basis")
CORE_SWAP = [(0, 1), (1, 0)]
HOP2 = (2, 1, 3, 0)
BF16 = jnp.bfloat16
F32 = jnp.float32
VMEM_LIMIT = 28 * 1024 * 1024


def device_id(x, y, z, core):
    return ((z % SIDE * SIDE + y % SIDE) * SIDE + x % SIDE) * 2 + core


def pairs(target):
    found = []
    for z in range(SIDE):
        for y in range(SIDE):
            for x in range(SIDE):
                for core in range(2):
                    found.append((device_id(x, y, z, core), device_id(*target(x, y, z, core))))
    assert len({to for _, to in found}) == len(found)
    return found


def hop1_pairs(step):
    return pairs(lambda x, y, z, core: (x + step, y, z, 0) if core == 0 else (x, y + step, z, 1))


def hop2_pairs(step):
    return pairs(lambda x, y, z, core: (x, y, z + step, core))


MATCHED = ((0, 0), (2, 1), (2, 0), (0, 1))
UNMATCHED = ((1, 1), (1, 0), (3, 1), (3, 0))


def hop3_pairs(send):
    def target(x, y, z, core):
        step, half = (MATCHED if (x + y + z) % 2 == core else UNMATCHED)[send]
        return (x, y + step, z, half) if core == 0 else (x + step, y, z, half)

    return pairs(target)


def coordinates():
    chip = lax.axis_index("shard")
    return chip % SIDE, chip // SIDE % SIDE, chip // (SIDE * SIDE), lax.axis_index("basis")


def group_of(x, y, z, kind, which):
    y_end = 2 * which + (x + z) % 2
    x_end = 2 * which + (y + z + 1) % 2
    return jnp.where(kind == 0, (z * SIDE + y_end) * SIDE + x, (z * SIDE + y) * SIDE + x_end)


def notes_kernel(blocks, counts_ref, dests_ref, rels_ref, lists_ref, out_ref):
    rows = CHIPS * 8
    x, y, z, _ = coordinates()
    counts = counts_ref[...]
    before = (
        lax.broadcasted_iota(jnp.int32, (CHIPS, CHIPS), 0)
        < lax.broadcasted_iota(jnp.int32, (CHIPS, CHIPS), 1)
    ).astype(F32)
    used = jnp.broadcast_to(counts.astype(F32), (8, CHIPS))
    rank = jnp.dot(used, before, preferred_element_type=F32)[:1]
    where = jnp.where(counts > 0, rank, -1.0).astype(jnp.int32)
    row = lax.broadcasted_iota(jnp.int32, (rows, 1), 0)
    slot, place = row // 8, row % 8
    line = place % SIDE
    owner = jnp.where(
        (x + y + z) % 2 == 0,
        slot // SIDE * SIDE + line,
        slot // 16 * 16 + line * SIDE + slot % SIDE,
    )

    def lookup(values, index):
        lane = lax.broadcasted_iota(jnp.int32, (rows, values.shape[1]), 1)
        return jnp.sum(jnp.where(lane == index, values, 0), axis=1, keepdims=True)

    position = lookup(where, owner)
    hit = (position == lax.broadcasted_iota(jnp.int32, (rows, blocks), 1)).astype(BF16)
    dests = jnp.concatenate([dests_ref[:, p * BROWS : (p + 1) * BROWS] for p in range(blocks)], axis=0)
    dests = jnp.dot(hit, dests.astype(BF16), preferred_element_type=F32).astype(jnp.int32)
    codes = jnp.where(position < 0, -1, dests + jnp.where(position >= blocks // 2, DST, 0))
    block = lookup(jnp.where(counts > 0, lists_ref[...], -1), slot)
    lane = lax.broadcasted_iota(jnp.int32, (rows, DST), 1)
    other = jnp.where(lane == 0, codes, block)
    for tile in range(BROWS // TILE):
        rel = lookup(rels_ref[...], position * (BROWS // TILE) + tile)
        other = jnp.where(lane == 1 + tile, rel, other)
    out_ref[...] = jnp.where(place < SIDE, codes, other)


def make_notes(counts, dests, rels, lists):
    vmem = pl.BlockSpec(memory_space=pltpu.VMEM)
    return pl.pallas_call(
        functools.partial(notes_kernel, dests.shape[1] // BROWS),
        out_shape=jax.ShapeDtypeStruct((CHIPS * 8, DST), jnp.int32),
        in_specs=[vmem] * 4,
        out_specs=vmem,
        name="notes",
    )(counts, dests, rels, lists).reshape(CHIPS, 8, DST)


WORDS = 4
HOP1 = (1, 3, 2)


def word(words_ref, group, line, which):
    return words_ref[(group * SIDE + line) * WORDS + which]


def reached(step, step_z, kind, which):
    x, y, z, _ = coordinates()
    x_to = jnp.where(kind == 0, (x + step) % SIDE, x)
    y_to = jnp.where(kind == 0, y, (y + step) % SIDE)
    return group_of(x_to, y_to, (z + step_z) % SIDE, kind, which)


def local_block(words_ref, table_ref, group):
    block = word(words_ref, group, 0, WORDS - 1)
    start = pl.multiple_of(jnp.maximum(block, 0) * BROWS, BROWS)
    return block >= 0, table_ref.at[pl.ds(start, BROWS)]


def run_moves(moves):
    for live, loads, _ in moves:

        @pl.when(live)
        def _(loads=loads):
            for load in loads:
                load.start()

    for live, loads, store in moves:

        @pl.when(live)
        def _(loads=loads, store=store):
            for load in loads:
                load.wait()
            store.start()

    for live, _, store in moves:
        pl.when(live)(store.wait)


def cross_kernel(steps_z, words_ref, table_ref, out_ref, held, sems):
    core = lax.axis_index("basis")
    moves = []
    for i, step_z in enumerate(steps_z):
        for step in range(SIDE):
            for which in range(2):
                live, source = local_block(words_ref, table_ref, reached(step, step_z, 1 - core, which))
                at = (i, step, which)
                load = pltpu.make_async_copy(source, held.at[at], sems.at[(0, *at)])
                store = pltpu.make_async_copy(held.at[at], out_ref.at[at], sems.at[(1, *at)])
                moves.append((live, (load,), store))
    run_moves(moves)


def cross(steps_z, words, table):
    shape = (len(steps_z), SIDE, 2, BROWS, table.shape[1])
    anywhere = pl.BlockSpec(memory_space=pl.ANY)
    return pl.pallas_call(
        functools.partial(cross_kernel, steps_z),
        out_shape=jax.ShapeDtypeStruct(shape, BF16),
        in_specs=[pl.BlockSpec(memory_space=pltpu.SMEM), anywhere],
        out_specs=anywhere,
        scratch_shapes=[pltpu.VMEM(shape, BF16), pltpu.SemaphoreType.DMA((2, len(steps_z), SIDE, 2))],
        cost_estimate=pl.CostEstimate(flops=0, bytes_accessed=len(steps_z) * 4 * 2**20, transcendentals=0),
        name="cross",
    )(words, table)


def pick_kernel(step_z, row, words_ref, table_ref, crossed_ref, *rest):
    outs, (held, sems) = rest[: len(HOP1)], rest[len(HOP1) :]
    core = lax.axis_index("basis")
    moves = []
    for i, step in enumerate(HOP1):
        for which in range(2):
            live, source = local_block(words_ref, table_ref, reached(step, step_z, core, which))
            loads = (
                pltpu.make_async_copy(source, held.at[i, which, 0], sems.at[0, i, which]),
                pltpu.make_async_copy(crossed_ref.at[row, step, which], held.at[i, which, 1], sems.at[1, i, which]),
            )
            store = pltpu.make_async_copy(held.at[i, which], outs[i].at[which], sems.at[2, i, which])
            moves.append((live, loads, store))
    run_moves(moves)


def pick(step_z, row, words, table, crossed):
    shape = (2, 2, BROWS, table.shape[1])
    anywhere = pl.BlockSpec(memory_space=pl.ANY)
    return pl.pallas_call(
        functools.partial(pick_kernel, step_z, row),
        out_shape=[jax.ShapeDtypeStruct(shape, BF16)] * len(HOP1),
        in_specs=[pl.BlockSpec(memory_space=pltpu.SMEM), anywhere, anywhere],
        out_specs=[anywhere] * len(HOP1),
        scratch_shapes=[
            pltpu.VMEM((len(HOP1), *shape), BF16),
            pltpu.SemaphoreType.DMA((3, len(HOP1), 2)),
        ],
        cost_estimate=pl.CostEstimate(flops=0, bytes_accessed=4 * 2**20, transcendentals=0),
        name="pick",
    )(words, table, crossed)


def project_kernel(step_z, row, words_ref, notes_ref, coeffs_ref, table_ref, crossed_ref, *rest):
    received, rest = rest[: len(HOP1)], rest[len(HOP1) :]
    own_basis, other_basis, out_ref, rows, notes, coeffs, total, basis, sems, coef_sems, more_sems = rest
    x, y, z, core = coordinates()
    width = table_ref.shape[1]
    along = jnp.where(core == 0, x, y)
    loads = [
        pltpu.make_async_copy(own_basis, basis.at[0], more_sems.at[0]),
        pltpu.make_async_copy(other_basis, basis.at[1], more_sems.at[1]),
    ]
    pieces, note_loads = [], []
    for which in range(2):
        group = reached(0, step_z, core, which)
        note_loads.append(pltpu.make_async_copy(notes_ref.at[group], notes.at[which], more_sems.at[2 + which]))
        note_loads[-1].start()
        for step in range(SIDE):
            line = (along - step) % SIDE
            code = word(words_ref, group, line, 0)
            rels = [word(words_ref, group, line, 1 + tile) for tile in range(2)]
            copies = [
                pltpu.make_async_copy(
                    coeffs_ref.at[rels[tile] // DST], coeffs.at[which, step, tile], coef_sems.at[which, step, tile]
                )
                for tile in range(2)
            ]
            if step == 0:
                _, source = local_block(words_ref, table_ref, group)
                sources = (source, crossed_ref.at[row, 0, which])
                copies += [
                    pltpu.make_async_copy(source, rows.at[which, step, part], sems.at[which, step, part])
                    for part, source in enumerate(sources)
                ]
            else:
                source = received[HOP1.index(step)].at[which]
                copies.append(pltpu.make_async_copy(source, rows.at[which, step], sems.at[which, step, 0]))

            @pl.when(code >= 0)
            def _(copies=copies):
                for copy in copies:
                    copy.start()

            pieces.append((which, step, line, code, rels, copies))
    for load in loads:
        load.start()
    total[...] = jnp.zeros_like(total)
    for load in note_loads:
        load.wait()
    lane = lax.broadcasted_iota(jnp.int32, (2, BROWS), 1)
    dest = lax.broadcasted_iota(jnp.int32, (DST, BROWS), 0)
    for which, step, line, code, rels, copies in pieces:

        @pl.when(code >= 0)
        def _(which=which, step=step, line=line, code=code, rels=rels, copies=copies):
            for copy in copies:
                copy.wait()
            half = jnp.where(code >= DST, 1, 0)
            hit = notes[which, pl.ds(line, 1), :] - half * DST == dest
            coef = [
                jnp.sum(
                    jnp.where(lane == rels[tile] % DST, coeffs[which, step, tile], 0.0), axis=1, keepdims=True
                )
                for tile in range(2)
            ]
            weights = jnp.where(lane < TILE, coef[0], coef[1])
            chosen = []
            for k in range(2):
                weight = jnp.where(core == 0, weights[k : k + 1], weights[1 - k : 2 - k])
                high = weight.astype(BF16).astype(F32)
                high, low = jnp.where(hit, high, 0.0), jnp.where(hit, weight - high, 0.0)
                chosen.append(jnp.concatenate([high, low], axis=1))
            chosen = jnp.concatenate(chosen, axis=0).astype(BF16)
            for part in range(2):
                block = rows[which, step, part]
                added = jnp.dot(
                    chosen, jnp.concatenate([block, block], axis=0), preferred_element_type=F32
                )
                column = pl.multiple_of(jnp.where(core == part, 0, width), width)
                total[which, half, :, pl.ds(column, width)] += added

    for load in loads:
        load.wait()
    summed = [
        total[:, :, k * DST : (k + 1) * DST, :].reshape(4 * DST, 2 * width).astype(BF16) for k in range(2)
    ]
    wide = basis.shape[2]
    tile = 256
    for start in range(0, wide, tile):
        result = jnp.dot(summed[0], basis[0, :, start : start + tile], preferred_element_type=F32)
        result += jnp.dot(summed[1], basis[1, :, start : start + tile], preferred_element_type=F32)
        out_ref[:, :, start : start + tile] = result.reshape(4, DST, tile).astype(BF16)


def project(step_z, row, words, notes, coeffs, table, crossed, received, own_basis, other_basis):
    width = table.shape[1]
    wide = own_basis.shape[1]
    anywhere = pl.BlockSpec(memory_space=pl.ANY)
    return pl.pallas_call(
        functools.partial(project_kernel, step_z, row),
        out_shape=jax.ShapeDtypeStruct((4, DST, wide), BF16),
        in_specs=[pl.BlockSpec(memory_space=pltpu.SMEM)] + [anywhere] * (6 + len(HOP1)),
        out_specs=pl.BlockSpec(memory_space=pltpu.VMEM),
        scratch_shapes=[
            pltpu.VMEM((2, SIDE, 2, BROWS, width), BF16),
            pltpu.VMEM((2, 8, DST), jnp.int32),
            pltpu.VMEM((2, SIDE, 2, 2, DST), F32),
            pltpu.VMEM((2, 2, 2 * DST, 2 * width), F32),
            pltpu.VMEM((2, 2 * width, wide), BF16),
            pltpu.SemaphoreType.DMA((2, SIDE, 2)),
            pltpu.SemaphoreType.DMA((2, SIDE, 2)),
            pltpu.SemaphoreType.DMA((4,)),
        ],
        cost_estimate=pl.CostEstimate(
            flops=2 * 4 * DST * 4 * width * wide, bytes_accessed=16 * 2**20, transcendentals=0
        ),
        compiler_params=pltpu.CompilerParams(vmem_limit_bytes=VMEM_LIMIT),
        name="project",
    )(words, notes, coeffs, table, crossed, *received, own_basis, other_basis)


def merge_kernel(order_ref, *refs):
    ins, outs = refs[:SIDE], refs[SIDE:]
    for send in range(4):
        at = order_ref[send]
        result = ins[0][at].astype(F32)
        for other in ins[1:]:
            result += other[at].astype(F32)
        outs[send][...] = result.astype(BF16)


def merge(order, parts):
    wide = parts[0].shape[2]
    slab = 32
    return pl.pallas_call(
        merge_kernel,
        out_shape=[jax.ShapeDtypeStruct((DST, wide), BF16)] * 4,
        grid_spec=pltpu.PrefetchScalarGridSpec(
            num_scalar_prefetch=1,
            grid=(DST // slab,),
            in_specs=[pl.BlockSpec((4, slab, wide), lambda i, order: (0, i, 0))] * SIDE,
            out_specs=[pl.BlockSpec((slab, wide), lambda i, order: (i, 0))] * 4,
        ),
        compiler_params=pltpu.CompilerParams(vmem_limit_bytes=VMEM_LIMIT),
        name="merge",
    )(order, *parts)


def body(features, bases, coeffs, block_lists, block_counts, tile_rel, dest_ids):
    x, y, z, core = coordinates()
    blocks = tile_rel.shape[1] * TILE // BROWS
    other_basis = lax.ppermute(bases[0], "basis", CORE_SWAP)

    sent = make_notes(block_counts, dest_ids, tile_rel, block_lists.reshape(1, CHIPS))
    notes = lax.all_to_all(sent, "shard", split_axis=0, concat_axis=0, tiled=True)
    words = notes[:, SIDE:, :WORDS].reshape(-1)
    rels = -(-coeffs.shape[0] // DST) * DST
    table = jnp.pad(coeffs.T, ((0, 0), (0, rels - coeffs.shape[0]))).reshape(2, -1, DST).transpose(1, 0, 2)

    groups = HOP2[:1], HOP2[1:]
    crossed = [lax.ppermute(cross(steps, words, features), "basis", CORE_SWAP) for steps in groups]
    crossed = {s: (steps.index(s), buf) for steps, buf in zip(groups, crossed) for s in steps}

    def send(step_z, words):
        picked = pick(step_z, crossed[step_z][0], words, features, crossed[step_z][1])
        return [lax.ppermute(buf, AXES, hop1_pairs(step)) for step, buf in zip(HOP1, picked)]

    arrived = [send(step_z, words) for step_z in HOP2[:2]]
    parts = []
    for i, step_z in enumerate(HOP2):
        row, buf = crossed[step_z]
        part = project(step_z, row, words, notes, table, features, buf, arrived[i], bases[0], other_basis)
        if i + 2 < len(HOP2):
            later, part = lax.optimization_barrier((words, part))
            arrived.append(send(HOP2[i + 2], later))
        parts.append(part if step_z == 0 else lax.ppermute(part, AXES, hop2_pairs(step_z)))

    last = jnp.where(core == 0, y, x)
    matched = (x + y + z) % 2 == core
    order = jnp.stack(
        [
            jnp.where(matched, (last + a) % SIDE // 2 * 2 + b, (last + c) % SIDE // 2 * 2 + d)
            for (a, b), (c, d) in zip(MATCHED, UNMATCHED)
        ]
    )
    merged = merge(order, parts)
    ends = [lax.ppermute(buf, AXES, hop3_pairs(send)) for send, buf in enumerate(merged)]
    summed = sum(end.astype(F32) for end in ends)

    rows_dev = blocks // 2 * BROWS
    my_dests = lax.dynamic_slice_in_dim(dest_ids[0], core * rows_dev, rows_dev)
    indegree = jnp.sum(
        (my_dests[None, :] == jnp.arange(DST, dtype=jnp.int32)[:, None]).astype(F32), axis=1
    )
    return (summed / jnp.maximum(indegree, 1.0)[:, None]).astype(BF16)


def solution(mesh):
    placed = (
        P("shard", "basis"),
        P("basis", None, None),
        P(),
        P("shard", None, None),
        P("shard", None),
        P("shard", None),
        P("shard", None),
    )
    return jax.shard_map(
        body, mesh=mesh, in_specs=placed, out_specs=P(("shard", "basis"), None), check_vma=False
    )
```

```python
import functools

import jax
import jax.numpy as jnp
from jax import lax
from jax.experimental import pallas as pl
from jax.experimental.pallas import tpu as pltpu
from jax.sharding import PartitionSpec as P

BROWS = 128
TILE = 64
DST = 128
SIDE = 4
CHIPS = SIDE**3
AXES = ("shard", "basis")
CORE_SWAP = [(0, 1), (1, 0)]
HOP2 = (2, 1, 3, 0)
BF16 = jnp.bfloat16
F32 = jnp.float32
SMALL = pl.CostEstimate(flops=1, bytes_accessed=1, transcendentals=0)
VMEM_SMALL = 2 * 1024 * 1024
VMEM_LIMIT = 22 * 1024 * 1024


def device_id(x, y, z, core):
    return ((z % SIDE * SIDE + y % SIDE) * SIDE + x % SIDE) * 2 + core


def pairs(target):
    found = []
    for z in range(SIDE):
        for y in range(SIDE):
            for x in range(SIDE):
                for core in range(2):
                    found.append((device_id(x, y, z, core), device_id(*target(x, y, z, core))))
    assert len({to for _, to in found}) == len(found)
    return found


def hop1_pairs(step):
    return pairs(lambda x, y, z, core: (x + step, y, z, 0) if core == 0 else (x, y + step, z, 1))


def hop2_pairs(step):
    return pairs(lambda x, y, z, core: (x, y, z + step, core))


MATCHED = ((0, 0), (2, 1), (2, 0), (0, 1))
UNMATCHED = ((1, 1), (1, 0), (3, 1), (3, 0))


def hop3_pairs(send):
    def target(x, y, z, core):
        step, half = (MATCHED if (x + y + z) % 2 == core else UNMATCHED)[send]
        return (x, y + step, z, half) if core == 0 else (x + step, y, z, half)

    return pairs(target)


def coordinates():
    chip = lax.axis_index("shard")
    return chip % SIDE, chip // SIDE % SIDE, chip // (SIDE * SIDE), lax.axis_index("basis")


def group_of(x, y, z, kind, which):
    y_end = 2 * which + (x + z) % 2
    x_end = 2 * which + (y + z + 1) % 2
    return jnp.where(kind == 0, (z * SIDE + y_end) * SIDE + x, (z * SIDE + y) * SIDE + x_end)


def notes_kernel(blocks, counts_ref, dests_ref, rels_ref, lists_ref, out_ref):
    rows = CHIPS * 8
    x, y, z, _ = coordinates()
    counts = counts_ref[...]
    before = (
        lax.broadcasted_iota(jnp.int32, (CHIPS, CHIPS), 0)
        < lax.broadcasted_iota(jnp.int32, (CHIPS, CHIPS), 1)
    ).astype(F32)
    used = jnp.broadcast_to(counts.astype(F32), (8, CHIPS))
    rank = jnp.dot(used, before, preferred_element_type=F32)[:1]
    where = jnp.where(counts > 0, rank, -1.0).astype(jnp.int32)
    row = lax.broadcasted_iota(jnp.int32, (rows, 1), 0)
    slot, place = row // 8, row % 8
    line = place % SIDE
    owner = jnp.where(
        (x + y + z) % 2 == 0,
        slot // SIDE * SIDE + line,
        slot // 16 * 16 + line * SIDE + slot % SIDE,
    )

    def lookup(values, index):
        lane = lax.broadcasted_iota(jnp.int32, (rows, values.shape[1]), 1)
        return jnp.sum(jnp.where(lane == index, values, 0), axis=1, keepdims=True)

    position = lookup(where, owner)
    hit = (position == lax.broadcasted_iota(jnp.int32, (rows, blocks), 1)).astype(BF16)
    dests = jnp.concatenate([dests_ref[:, p * BROWS : (p + 1) * BROWS] for p in range(blocks)], axis=0)
    dests = jnp.dot(hit, dests.astype(BF16), preferred_element_type=F32).astype(jnp.int32)
    codes = jnp.where(position < 0, -1, dests + jnp.where(position >= blocks // 2, DST, 0))
    block = lookup(jnp.where(counts > 0, lists_ref[...], -1), slot)
    lane = lax.broadcasted_iota(jnp.int32, (rows, DST), 1)
    other = jnp.where(lane == 0, codes, block)
    for tile in range(BROWS // TILE):
        rel = lookup(rels_ref[...], position * (BROWS // TILE) + tile)
        other = jnp.where(lane == 1 + tile, rel, other)
    out_ref[...] = jnp.where(place < SIDE, codes, other)


def make_notes(counts, dests, rels, lists):
    vmem = pl.BlockSpec(memory_space=pltpu.VMEM)
    return pl.pallas_call(
        functools.partial(notes_kernel, dests.shape[1] // BROWS),
        out_shape=jax.ShapeDtypeStruct((CHIPS * 8, DST), jnp.int32),
        in_specs=[vmem] * 4,
        out_specs=vmem,
        compiler_params=pltpu.CompilerParams(vmem_limit_bytes=VMEM_LIMIT),
        name="notes",
    )(counts, dests, rels, lists).reshape(CHIPS, 8, DST)


WORDS = 4
HOP1 = (1, 3, 2)


def word(words_ref, group, line, which):
    return words_ref[(group * SIDE + line) * WORDS + which]


def reached(step, step_z, kind, which):
    x, y, z, _ = coordinates()
    x_to = jnp.where(kind == 0, (x + step) % SIDE, x)
    y_to = jnp.where(kind == 0, y, (y + step) % SIDE)
    return group_of(x_to, y_to, (z + step_z) % SIDE, kind, which)


def local_block(words_ref, table_ref, group):
    block = word(words_ref, group, 0, WORDS - 1)
    start = pl.multiple_of(jnp.maximum(block, 0) * BROWS, BROWS)
    return block >= 0, table_ref.at[pl.ds(start, BROWS)]


def run_moves(moves):
    for live, copies in moves:

        @pl.when(live)
        def _(copies=copies):
            for copy in copies:
                copy.start()

    for live, copies in moves:

        @pl.when(live)
        def _(copies=copies):
            for copy in copies:
                copy.wait()


def in_hbm(array):
    return pltpu.with_memory_space_constraint(array, pltpu.HBM)


def in_vmem(array):
    return pltpu.with_memory_space_constraint(array, pltpu.VMEM)


SMEM_SPEC = pl.BlockSpec(memory_space=pltpu.SMEM)
HBM_SPEC = pl.BlockSpec(memory_space=pltpu.HBM)
VMEM_SPEC = pl.BlockSpec(memory_space=pltpu.VMEM)


def cross_kernel(steps_z, words_ref, table_ref, out_ref, sems):
    core = lax.axis_index("basis")
    moves = []
    for i, step_z in enumerate(steps_z):
        for step in range(SIDE):
            for which in range(2):
                live, source = local_block(words_ref, table_ref, reached(step, step_z, 1 - core, which))
                at = (i, step, which)
                moves.append((live, (pltpu.make_async_copy(source, out_ref.at[at], sems.at[at]),)))
    run_moves(moves)


def cross(steps_z, words, table):
    shape = (len(steps_z), SIDE, 2, BROWS, table.shape[1])
    return pl.pallas_call(
        functools.partial(cross_kernel, steps_z),
        out_shape=pltpu.VMEM(shape, BF16),
        in_specs=[SMEM_SPEC, HBM_SPEC],
        out_specs=VMEM_SPEC,
        scratch_shapes=[pltpu.SemaphoreType.DMA((len(steps_z), SIDE, 2))],
        compiler_params=pltpu.CompilerParams(vmem_limit_bytes=VMEM_SMALL),
        cost_estimate=SMALL,
        name="cross",
    )(words, in_hbm(table))


def pick_kernel(step_z, row, words_ref, table_ref, crossed_ref, *rest):
    outs, sems = rest[: len(HOP1)], rest[len(HOP1)]
    core = lax.axis_index("basis")
    moves = []
    for i, step in enumerate(HOP1):
        for which in range(2):
            live, source = local_block(words_ref, table_ref, reached(step, step_z, core, which))
            copies = (
                pltpu.make_async_copy(source, outs[i].at[which, 0], sems.at[0, i, which]),
                pltpu.make_async_copy(crossed_ref.at[row, step, which], outs[i].at[which, 1], sems.at[1, i, which]),
            )
            moves.append((live, copies))
    run_moves(moves)


def pick(step_z, row, words, table, crossed):
    return pl.pallas_call(
        functools.partial(pick_kernel, step_z, row),
        out_shape=[pltpu.VMEM((2, 2, BROWS, table.shape[1]), BF16)] * len(HOP1),
        in_specs=[SMEM_SPEC, HBM_SPEC, VMEM_SPEC],
        out_specs=[VMEM_SPEC] * len(HOP1),
        scratch_shapes=[pltpu.SemaphoreType.DMA((2, len(HOP1), 2))],
        compiler_params=pltpu.CompilerParams(vmem_limit_bytes=VMEM_SMALL),
        cost_estimate=SMALL,
        name="pick",
    )(words, in_hbm(table), in_vmem(crossed))


def project_kernel(step_z, row, words_ref, table_ref, notes_ref, coeffs_ref, crossed_ref, *rest):
    received, rest = rest[: len(HOP1)], rest[len(HOP1) :]
    own_basis, other_basis, out_ref, local, total, sems = rest
    x, y, z, core = coordinates()
    width = table_ref.shape[1]
    along = jnp.where(core == 0, x, y)
    pieces = []
    for which in range(2):
        group = reached(0, step_z, core, which)
        for step in HOP1 + (0,):
            line = (along - step) % SIDE
            code = word(words_ref, group, line, 0)
            rels = [word(words_ref, group, line, 1 + tile) for tile in range(2)]
            copy = None
            if step == 0:
                copy = pltpu.make_async_copy(
                    local_block(words_ref, table_ref, group)[1], local.at[which], sems.at[which]
                )
                pl.when(code >= 0)(copy.start)
            pieces.append((which, step, group, line, code, rels, copy))
    total[...] = jnp.zeros_like(total)
    lane = lax.broadcasted_iota(jnp.int32, (2, BROWS), 1)
    dest = lax.broadcasted_iota(jnp.int32, (DST, BROWS), 0)
    for which, step, group, line, code, rels, copy in pieces:

        @pl.when(code >= 0)
        def _(which=which, step=step, group=group, line=line, code=code, rels=rels, copy=copy):
            half = jnp.where(code >= DST, 1, 0)
            hit = notes_ref[group, pl.ds(line, 1), :] - half * DST == dest
            coef = [
                jnp.sum(
                    jnp.where(lane == rels[tile] % DST, coeffs_ref[rels[tile] // DST], 0.0), axis=1, keepdims=True
                )
                for tile in range(2)
            ]
            weights = jnp.where(lane < TILE, coef[0], coef[1])
            chosen = []
            for k in range(2):
                weight = jnp.where(core == 0, weights[k : k + 1], weights[1 - k : 2 - k])
                high = weight.astype(BF16).astype(F32)
                high, low = jnp.where(hit, high, 0.0), jnp.where(hit, weight - high, 0.0)
                chosen.append(jnp.concatenate([high, low], axis=1))
            chosen = jnp.concatenate(chosen, axis=0).astype(BF16)
            for part in range(2):
                if step > 0:
                    block = received[HOP1.index(step)][which, part]
                elif part == 1:
                    block = crossed_ref[row, 0, which]
                else:
                    copy.wait()
                    block = local[which]
                added = jnp.dot(
                    chosen, jnp.concatenate([block, block], axis=0), preferred_element_type=F32
                )
                column = pl.multiple_of(jnp.where(core == part, 0, width), width)
                total[which, half, :, pl.ds(column, width)] += added

    summed = [
        total[:, :, k * DST : (k + 1) * DST, :].reshape(4 * DST, 2 * width).astype(BF16) for k in range(2)
    ]
    wide = own_basis.shape[1]
    tile = 256
    for start in range(0, wide, tile):
        result = jnp.dot(summed[0], own_basis[:, start : start + tile], preferred_element_type=F32)
        result += jnp.dot(summed[1], other_basis[:, start : start + tile], preferred_element_type=F32)
        out_ref[:, :, start : start + tile] = result.reshape(4, DST, tile).astype(BF16)


def project(step_z, row, words, table, *others):
    width = table.shape[1]
    wide = others[-1].shape[1]
    return pl.pallas_call(
        functools.partial(project_kernel, step_z, row),
        out_shape=pltpu.VMEM((4, DST, wide), BF16),
        in_specs=[SMEM_SPEC, HBM_SPEC] + [VMEM_SPEC] * len(others),
        out_specs=VMEM_SPEC,
        scratch_shapes=[
            pltpu.VMEM((2, BROWS, width), BF16),
            pltpu.VMEM((2, 2, 2 * DST, 2 * width), F32),
            pltpu.SemaphoreType.DMA((2,)),
        ],
        cost_estimate=SMALL,
        compiler_params=pltpu.CompilerParams(vmem_limit_bytes=VMEM_LIMIT),
        name="project",
    )(words, in_hbm(table), *map(in_vmem, others))


def merge_kernel(order_ref, *refs):
    ins, outs = refs[:SIDE], refs[SIDE:]
    for send in range(4):
        at = order_ref[send]
        result = ins[0][at].astype(F32)
        for other in ins[1:]:
            result += other[at].astype(F32)
        outs[send][...] = result.astype(BF16)


def merge(order, parts):
    return pl.pallas_call(
        merge_kernel,
        out_shape=[pltpu.VMEM(parts[0].shape[1:], BF16)] * 4,
        in_specs=[SMEM_SPEC] + [VMEM_SPEC] * SIDE,
        out_specs=[VMEM_SPEC] * 4,
        compiler_params=pltpu.CompilerParams(vmem_limit_bytes=VMEM_LIMIT),
        cost_estimate=SMALL,
        name="merge",
    )(order, *map(in_vmem, parts))


def body(features, bases, coeffs, block_lists, block_counts, tile_rel, dest_ids):
    x, y, z, core = coordinates()
    blocks = tile_rel.shape[1] * TILE // BROWS
    other_basis = lax.ppermute(bases[0], "basis", CORE_SWAP)

    sent = make_notes(block_counts, dest_ids, tile_rel, block_lists.reshape(1, CHIPS))
    notes = lax.all_to_all(sent, "shard", split_axis=0, concat_axis=0, tiled=True)
    words = notes[:, SIDE:, :WORDS].reshape(-1)
    rels = -(-coeffs.shape[0] // DST) * DST
    table = jnp.pad(coeffs.T, ((0, 0), (0, rels - coeffs.shape[0]))).reshape(2, -1, DST).transpose(1, 0, 2)

    words, other_basis = lax.optimization_barrier((words, other_basis))
    groups = HOP2[:1], HOP2[1:]
    first = cross(groups[0], words, features)
    first, later = lax.optimization_barrier((first, words))
    second = cross(groups[1], later, features)
    first = lax.ppermute(first, "basis", CORE_SWAP)
    first, second = lax.optimization_barrier((first, second))
    crossed = first, lax.ppermute(second, "basis", CORE_SWAP)
    crossed = {s: (steps.index(s), buf) for steps, buf in zip(groups, crossed) for s in steps}

    arrived, parts, later = [], [], words
    for i, step_z in enumerate(HOP2):
        row, buf = crossed[step_z]
        picked = pick(step_z, row, later, features, buf)
        picked, later = lax.optimization_barrier((picked, later))
        if i > 0:
            picked, arrived[-1] = lax.optimization_barrier((picked, arrived[-1]))
        if i == 3:
            picked, parts[0] = lax.optimization_barrier((picked, parts[0]))
        arrived.append([lax.ppermute(buf, AXES, hop1_pairs(step)) for step, buf in zip(HOP1, picked)])
        part = project(step_z, row, words, features, notes, table, buf, *arrived[i], bases[0], other_basis)
        parts.append(part if step_z == 0 else lax.ppermute(part, AXES, hop2_pairs(step_z)))

    last = jnp.where(core == 0, y, x)
    matched = (x + y + z) % 2 == core
    order = jnp.stack(
        [
            jnp.where(matched, (last + a) % SIDE // 2 * 2 + b, (last + c) % SIDE // 2 * 2 + d)
            for (a, b), (c, d) in zip(MATCHED, UNMATCHED)
        ]
    )
    merged = merge(order, parts)
    ends = [lax.ppermute(buf, AXES, hop3_pairs(send)) for send, buf in enumerate(merged)]
    summed = sum(end.astype(F32) for end in ends)

    rows_dev = blocks // 2 * BROWS
    my_dests = lax.dynamic_slice_in_dim(dest_ids[0], core * rows_dev, rows_dev)
    indegree = jnp.sum(
        (my_dests[None, :] == jnp.arange(DST, dtype=jnp.int32)[:, None]).astype(F32), axis=1
    )
    return (summed / jnp.maximum(indegree, 1.0)[:, None]).astype(BF16)


def solution(mesh):
    placed = (
        P("shard", "basis"),
        P("basis", None, None),
        P(),
        P("shard", None, None),
        P("shard", None),
        P("shard", None),
        P("shard", None),
    )
    return jax.shard_map(
        body, mesh=mesh, in_specs=placed, out_specs=P(("shard", "basis"), None), check_vma=False
    )
```

```python
import functools

import jax
import jax.numpy as jnp
from jax import lax
from jax.experimental import pallas as pl
from jax.experimental.pallas import tpu as pltpu
from jax.sharding import PartitionSpec as P

BROWS = 128
TILE = 64
DST = 128
SIDE = 4
CHIPS = SIDE**3
AXES = ("shard", "basis")
CORE_SWAP = [(0, 1), (1, 0)]
CHUNKS = (((2, 0), (2, 1)), ((1, 0), (3, 0)), ((1, 1), (3, 1)), ((0, 0), (0, 1)))
FROM_BELOW, FROM_ABOVE = 1, 2
BF16 = jnp.bfloat16
F32 = jnp.float32
SMALL = pl.CostEstimate(flops=1, bytes_accessed=1, transcendentals=0)
VMEM_SMALL = 2 * 1024 * 1024
VMEM_LIMIT = 16 * 1024 * 1024


def device_id(x, y, z, core):
    return ((z % SIDE * SIDE + y % SIDE) * SIDE + x % SIDE) * 2 + core


def pairs(target):
    found = []
    for z in range(SIDE):
        for y in range(SIDE):
            for x in range(SIDE):
                for core in range(2):
                    found.append((device_id(x, y, z, core), device_id(*target(x, y, z, core))))
    assert len({to for _, to in found}) == len(found)
    return found


def hop1_pairs(step):
    return pairs(lambda x, y, z, core: (x + step, y, z, 0) if core == 0 else (x, y + step, z, 1))


def hop2_pairs(step):
    return pairs(lambda x, y, z, core: (x, y, z + step, core))


MATCHED = ((0, 0), (2, 1), (2, 0), (0, 1))
UNMATCHED = ((1, 1), (1, 0), (3, 1), (3, 0))


def hop3_pairs(send):
    def target(x, y, z, core):
        step, half = (MATCHED if (x + y + z) % 2 == core else UNMATCHED)[send]
        return (x, y + step, z, half) if core == 0 else (x + step, y, z, half)

    return pairs(target)


def coordinates():
    chip = lax.axis_index("shard")
    return chip % SIDE, chip // SIDE % SIDE, chip // (SIDE * SIDE), lax.axis_index("basis")


def group_of(x, y, z, kind, which):
    y_end = 2 * which + (x + z) % 2
    x_end = 2 * which + (y + z + 1) % 2
    return jnp.where(kind == 0, (z * SIDE + y_end) * SIDE + x, (z * SIDE + y) * SIDE + x_end)


def in_hbm(array):
    return pltpu.with_memory_space_constraint(array, pltpu.HBM)


def in_vmem(array):
    return pltpu.with_memory_space_constraint(array, pltpu.VMEM)


SMEM_SPEC = pl.BlockSpec(memory_space=pltpu.SMEM)
HBM_SPEC = pl.BlockSpec(memory_space=pltpu.HBM)
VMEM_SPEC = pl.BlockSpec(memory_space=pltpu.VMEM)


def notes_kernel(blocks, *refs):
    given, out_ref, held, sems = refs[:4], refs[4], refs[5:9], refs[9]
    copies = [pltpu.make_async_copy(a, b, sems.at[i]) for i, (a, b) in enumerate(zip(given, held))]
    for copy in copies:
        copy.start()
    for copy in copies:
        copy.wait()
    counts_ref, dests_ref, rels_ref, lists_ref = held
    rows = CHIPS * 8
    x, y, z, _ = coordinates()
    counts = counts_ref[...]
    before = (
        lax.broadcasted_iota(jnp.int32, (CHIPS, CHIPS), 0)
        < lax.broadcasted_iota(jnp.int32, (CHIPS, CHIPS), 1)
    ).astype(F32)
    used = jnp.broadcast_to(counts.astype(F32), (8, CHIPS))
    rank = jnp.dot(used, before, preferred_element_type=F32)[:1]
    where = jnp.where(counts > 0, rank, -1.0).astype(jnp.int32)
    row = lax.broadcasted_iota(jnp.int32, (rows, 1), 0)
    slot, place = row // 8, row % 8
    line = place % SIDE
    owner = jnp.where(
        (x + y + z) % 2 == 0,
        slot // SIDE * SIDE + line,
        slot // 16 * 16 + line * SIDE + slot % SIDE,
    )

    def lookup(values, index):
        lane = lax.broadcasted_iota(jnp.int32, (rows, values.shape[1]), 1)
        return jnp.sum(jnp.where(lane == index, values, 0), axis=1, keepdims=True)

    position = lookup(where, owner)
    hit = (position == lax.broadcasted_iota(jnp.int32, (rows, blocks), 1)).astype(BF16)
    dests = jnp.concatenate([dests_ref[:, p * BROWS : (p + 1) * BROWS] for p in range(blocks)], axis=0)
    dests = jnp.dot(hit, dests.astype(BF16), preferred_element_type=F32).astype(jnp.int32)
    codes = jnp.where(position < 0, -1, dests + jnp.where(position >= blocks // 2, DST, 0))
    block = lookup(jnp.where(counts > 0, lists_ref[...], -1), slot)
    lane = lax.broadcasted_iota(jnp.int32, (rows, DST), 1)
    other = jnp.where(lane == 0, codes, block)
    for tile in range(BROWS // TILE):
        rel = lookup(rels_ref[...], position * (BROWS // TILE) + tile)
        other = jnp.where(lane == 1 + tile, rel, other)
    out_ref[...] = jnp.where(place < SIDE, codes, other)


def make_notes(*given):
    return pl.pallas_call(
        functools.partial(notes_kernel, given[1].shape[1] // BROWS),
        out_shape=jax.ShapeDtypeStruct((CHIPS * 8, DST), jnp.int32),
        in_specs=[HBM_SPEC] * 4,
        out_specs=VMEM_SPEC,
        scratch_shapes=[pltpu.VMEM(array.shape, jnp.int32) for array in given] + [pltpu.SemaphoreType.DMA((4,))],
        compiler_params=pltpu.CompilerParams(vmem_limit_bytes=VMEM_LIMIT),
        name="notes",
    )(*map(in_hbm, given)).reshape(CHIPS, 8, DST)


WORDS = 4
HOP1 = (1, 3, 2)


def word(words_ref, group, line, which):
    return words_ref[(group * SIDE + line) * WORDS + which]


def reached(step, kind, step_z, which):
    x, y, z, _ = coordinates()
    x_to = jnp.where(kind == 0, (x + step) % SIDE, x)
    y_to = jnp.where(kind == 0, y, (y + step) % SIDE)
    return group_of(x_to, y_to, (z + step_z) % SIDE, kind, which)


def local_block(words_ref, table_ref, group):
    block = word(words_ref, group, 0, WORDS - 1)
    start = pl.multiple_of(jnp.maximum(block, 0) * BROWS, BROWS)
    return block >= 0, table_ref.at[pl.ds(start, BROWS)]


def run_moves(moves):
    for live, copies in moves:

        @pl.when(live)
        def _(copies=copies):
            for copy in copies:
                copy.start()

    for live, copies in moves:

        @pl.when(live)
        def _(copies=copies):
            for copy in copies:
                copy.wait()


def cross_kernel(chunks, words_ref, table_ref, out_ref, sems):
    core = lax.axis_index("basis")
    moves = []
    for i, chunk in enumerate(chunks):
        for step in range(SIDE):
            for pair, place in enumerate(chunk):
                live, source = local_block(words_ref, table_ref, reached(step, 1 - core, *place))
                at = (i, step, pair)
                moves.append((live, (pltpu.make_async_copy(source, out_ref.at[at], sems.at[at]),)))
    run_moves(moves)


def cross(chunks, words, table):
    shape = (len(chunks), SIDE, 2, BROWS, table.shape[1])
    return pl.pallas_call(
        functools.partial(cross_kernel, chunks),
        out_shape=pltpu.VMEM(shape, BF16),
        in_specs=[SMEM_SPEC, HBM_SPEC],
        out_specs=VMEM_SPEC,
        scratch_shapes=[pltpu.SemaphoreType.DMA((len(chunks), SIDE, 2))],
        compiler_params=pltpu.CompilerParams(vmem_limit_bytes=VMEM_SMALL),
        cost_estimate=SMALL,
        name="cross",
    )(words, in_hbm(table))


def pick_kernel(chunk, row, words_ref, table_ref, crossed_ref, *rest):
    outs, sems = rest[: len(HOP1)], rest[len(HOP1)]
    core = lax.axis_index("basis")
    moves = []
    for j, step in enumerate(HOP1):
        for pair, place in enumerate(chunk):
            live, source = local_block(words_ref, table_ref, reached(step, core, *place))
            copies = (
                pltpu.make_async_copy(source, outs[j].at[pair, 0], sems.at[0, j, pair]),
                pltpu.make_async_copy(crossed_ref.at[row, step, pair], outs[j].at[pair, 1], sems.at[1, j, pair]),
            )
            moves.append((live, copies))
    run_moves(moves)


def pick(chunk, row, words, table, crossed):
    return pl.pallas_call(
        functools.partial(pick_kernel, chunk, row),
        out_shape=[pltpu.VMEM((2, 2, BROWS, table.shape[1]), BF16)] * len(HOP1),
        in_specs=[SMEM_SPEC, HBM_SPEC, VMEM_SPEC],
        out_specs=[VMEM_SPEC] * len(HOP1),
        scratch_shapes=[pltpu.SemaphoreType.DMA((2, len(HOP1), 2))],
        compiler_params=pltpu.CompilerParams(vmem_limit_bytes=VMEM_SMALL),
        cost_estimate=SMALL,
        name="pick",
    )(words, in_hbm(table), in_vmem(crossed))


def project_kernel(chunk, row, added, words_ref, table_ref, own_basis, other_basis, notes_ref, coeffs_ref, crossed_ref, *rest):
    received, rest = rest[: len(HOP1)], rest[len(HOP1) :]
    extra, rest = rest[: len(added)], rest[len(added) :]
    outs, (local, total, sems) = rest[:2], rest[2:]
    x, y, z, core = coordinates()
    width = table_ref.shape[1]
    along = jnp.where(core == 0, x, y)
    pieces = []
    for which, place in enumerate(chunk):
        group = reached(0, core, *place)
        for step in HOP1 + (0,):
            line = (along - step) % SIDE
            code = word(words_ref, group, line, 0)
            rels = [word(words_ref, group, line, 1 + tile) for tile in range(2)]
            copy = None
            if step == 0:
                copy = pltpu.make_async_copy(
                    local_block(words_ref, table_ref, group)[1], local.at[which], sems.at[which]
                )
                pl.when(code >= 0)(copy.start)
            pieces.append((which, step, group, line, code, rels, copy))
    total[...] = jnp.zeros_like(total)
    lane = lax.broadcasted_iota(jnp.int32, (2, BROWS), 1)
    dest = lax.broadcasted_iota(jnp.int32, (DST, BROWS), 0)
    for which, step, group, line, code, rels, copy in pieces:

        @pl.when(code >= 0)
        def _(which=which, step=step, group=group, line=line, code=code, rels=rels, copy=copy):
            half = jnp.where(code >= DST, 1, 0)
            hit = notes_ref[group, pl.ds(line, 1), :] - half * DST == dest
            coef = [
                jnp.sum(
                    jnp.where(lane == rels[tile] % DST, coeffs_ref[rels[tile] // DST], 0.0), axis=1, keepdims=True
                )
                for tile in range(2)
            ]
            weights = jnp.where(lane < TILE, coef[0], coef[1])
            chosen = []
            for k in range(2):
                weight = jnp.where(core == 0, weights[k : k + 1], weights[1 - k : 2 - k])
                high = weight.astype(BF16).astype(F32)
                high, low = jnp.where(hit, high, 0.0), jnp.where(hit, weight - high, 0.0)
                chosen.append(jnp.concatenate([high, low], axis=1))
            chosen = jnp.concatenate(chosen, axis=0).astype(BF16)
            for part in range(2):
                if step > 0:
                    block = received[HOP1.index(step)][which, part]
                elif part == 1:
                    block = crossed_ref[row, 0, which]
                else:
                    copy.wait()
                    block = local[which]
                sums = jnp.dot(chosen, jnp.concatenate([block, block], axis=0), preferred_element_type=F32)
                column = pl.multiple_of(jnp.where(core == part, 0, width), width)
                total[which, half, :, pl.ds(column, width)] += sums

    summed = [
        total[:, :, k * DST : (k + 1) * DST, :].reshape(4 * DST, 2 * width).astype(BF16) for k in range(2)
    ]
    wide = own_basis.shape[1]
    tile = 256
    for start in range(0, wide, tile):
        result = jnp.dot(summed[0], own_basis[:, start : start + tile], preferred_element_type=F32)
        result += jnp.dot(summed[1], other_basis[:, start : start + tile], preferred_element_type=F32)
        result = result.reshape(2, 2, DST, tile)
        for which in range(2):
            here = result[which]
            if which in added:
                here += extra[added.index(which)][:, :, start : start + tile].astype(F32)
            outs[which][:, :, start : start + tile] = here.astype(BF16)


def project(chunk, row, added, words, table, *others):
    width = table.shape[1]
    wide = 2 * width
    return pl.pallas_call(
        functools.partial(project_kernel, chunk, row, added),
        out_shape=[pltpu.VMEM((2, DST, wide), BF16)] * 2,
        in_specs=[SMEM_SPEC, HBM_SPEC] + [VMEM_SPEC] * len(others),
        out_specs=[VMEM_SPEC] * 2,
        scratch_shapes=[
            pltpu.VMEM((2, BROWS, width), BF16),
            pltpu.VMEM((2, 2, 2 * DST, 2 * width), F32),
            pltpu.SemaphoreType.DMA((2,)),
        ],
        cost_estimate=pl.CostEstimate(flops=6 * 10**9, bytes_accessed=20 * 10**6, transcendentals=0),
        compiler_params=pltpu.CompilerParams(vmem_limit_bytes=VMEM_LIMIT),
        name="project",
    )(words, in_hbm(table), *map(in_vmem, others))


def merge_kernel(*refs):
    ins, outs = refs[:6], refs[6:]
    x, y, z, core = coordinates()
    last = jnp.where(core == 0, y, x)
    matched = (x + y + z) % 2 == core
    for send, ((step, to), (other_step, other_to)) in enumerate(zip(MATCHED, UNMATCHED)):
        which = (last + jnp.where(matched, step, other_step)) % SIDE // 2
        half = jnp.where(matched, to, other_to)
        for group in range(2):

            @pl.when(which == group)
            def _(group=group, half=half, send=send):
                result = ins[3 * group][half].astype(F32)
                for other in ins[3 * group + 1 : 3 * group + 3]:
                    result += other[half].astype(F32)
                outs[send][...] = result.astype(BF16)


def merge(parts):
    return pl.pallas_call(
        merge_kernel,
        out_shape=[pltpu.VMEM(parts[0].shape[1:], BF16)] * 4,
        in_specs=[VMEM_SPEC] * len(parts),
        out_specs=[VMEM_SPEC] * 4,
        compiler_params=pltpu.CompilerParams(vmem_limit_bytes=VMEM_LIMIT),
        cost_estimate=SMALL,
        name="merge",
    )(*map(in_vmem, parts))


def degree_kernel(dests_ref, out_ref):
    rows = dests_ref.shape[1] // 2
    mine = dests_ref[:, pl.ds(pl.multiple_of(lax.axis_index("basis") * rows, BROWS), rows)]
    hit = mine == lax.broadcasted_iota(jnp.int32, (DST, rows), 0)
    count = jnp.sum(jnp.where(hit, 1.0, 0.0), axis=1, keepdims=True)
    out_ref[...] = jnp.broadcast_to(jnp.maximum(count, 1.0), out_ref.shape)


def degrees(dests):
    return pl.pallas_call(
        degree_kernel,
        out_shape=pltpu.VMEM((DST, BROWS), F32),
        in_specs=[VMEM_SPEC],
        out_specs=VMEM_SPEC,
        compiler_params=pltpu.CompilerParams(vmem_limit_bytes=2 * VMEM_SMALL),
        cost_estimate=SMALL,
        name="degree",
    )(dests)


def table_kernel(coeffs_ref, out_ref):
    rels = coeffs_ref.shape[1]
    for i in range(out_ref.shape[0]):
        here = min(DST, rels - i * DST)
        out_ref[i, :, :here] = coeffs_ref[:, i * DST : i * DST + here]


def make_table(coeffs):
    rels = coeffs.shape[0]
    return pl.pallas_call(
        table_kernel,
        out_shape=pltpu.VMEM((-(-rels // DST), 2, DST), F32),
        in_specs=[VMEM_SPEC],
        out_specs=VMEM_SPEC,
        compiler_params=pltpu.CompilerParams(vmem_limit_bytes=2 * VMEM_SMALL),
        cost_estimate=SMALL,
        name="table",
    )(coeffs.T)


def finish_kernel(degree_ref, *refs):
    ends, out_ref = refs[:-1], refs[-1]
    degree = degree_ref[...]
    for start in range(0, out_ref.shape[1], BROWS):
        here = slice(start, start + BROWS)
        summed = ends[0][:, here].astype(F32)
        for end in ends[1:]:
            summed += end[:, here].astype(F32)
        out_ref[:, here] = (summed / degree).astype(BF16)


def finish(degree, ends):
    return pl.pallas_call(
        finish_kernel,
        out_shape=jax.ShapeDtypeStruct(ends[0].shape, BF16),
        in_specs=[VMEM_SPEC] * (1 + len(ends)),
        out_specs=VMEM_SPEC,
        compiler_params=pltpu.CompilerParams(vmem_limit_bytes=2 * VMEM_SMALL),
        cost_estimate=SMALL,
        name="finish",
    )(*map(in_vmem, (degree, *ends)))


def body(features, bases, coeffs, block_lists, block_counts, tile_rel, dest_ids):
    other_basis = lax.ppermute(bases[0], "basis", CORE_SWAP)

    sent = make_notes(block_counts, dest_ids, tile_rel, block_lists.reshape(1, CHIPS))
    notes = lax.all_to_all(sent, "shard", split_axis=0, concat_axis=0, tiled=True)
    words = notes[:, SIDE:, :WORDS].reshape(-1)
    table, degree = make_table(coeffs), degrees(dest_ids)

    words, other_basis = lax.optimization_barrier((words, other_basis))
    both = bases[0], other_basis

    first = cross(CHUNKS[:1], words, features)
    first, later = lax.optimization_barrier((first, words))
    second = cross(CHUNKS[1:], later, features)
    first = lax.ppermute(first, "basis", CORE_SWAP)
    first, second = lax.optimization_barrier((first, second))
    second = lax.ppermute(second, "basis", CORE_SWAP)
    crossed = [(0, first)] + [(i, second) for i in range(len(CHUNKS) - 1)]

    def pick_chunk(i, after):
        (row, buf), (ready, _) = crossed[i], lax.optimization_barrier((words, after))
        bufs = pick(CHUNKS[i], row, ready, features, buf)
        return lax.optimization_barrier((bufs, words))

    picked, ready = [pick_chunk(0, words)[0]], words
    bufs, _ = pick_chunk(1, picked[0])
    picked.append(bufs)
    arrived, parts = [], []
    for i, (chunk, (row, buf)) in enumerate(zip(CHUNKS, crossed)):
        came = []
        for j, step in enumerate(HOP1):
            sent = picked[i][j]
            if i > 0:
                sent, arrived[-1][j] = lax.optimization_barrier((sent, arrived[-1][j]))
            came.append(lax.ppermute(sent, AXES, hop1_pairs(step)))
        arrived.append(came)
        given = [ready, features, *both, notes, table, buf, *came]
        added = ()
        if i == FROM_BELOW:
            added, given = (0,), given + [parts[0][0]]
        if i == FROM_ABOVE:
            added, given = (1,), given + [parts[0][1]]
        part = project(chunk, row, added, *given)
        if i + 2 < len(CHUNKS):
            bufs, ready = pick_chunk(i + 2, part)
            picked.append(bufs)
        if i < len(CHUNKS) - 1:
            part = [lax.ppermute(p, AXES, hop2_pairs(step)) for p, step in zip(part, (1, 3))]
        parts.append(part)
    parts = [parts[3][0], *parts[1], parts[3][1], *parts[2]]

    merged = merge(parts)
    ends = [lax.ppermute(buf, AXES, hop3_pairs(send)) for send, buf in enumerate(merged)]
    return finish(degree, ends)


def solution(mesh):
    placed = (
        P("shard", "basis"),
        P("basis", None, None),
        P(),
        P("shard", None, None),
        P("shard", None),
        P("shard", None),
        P("shard", None),
    )
    return jax.shard_map(
        body, mesh=mesh, in_specs=placed, out_specs=P(("shard", "basis"), None), check_vma=False
    )
```

```python
import functools

import jax
import jax.numpy as jnp
from jax import lax
from jax.experimental import pallas as pl
from jax.experimental.pallas import tpu as pltpu
from jax.sharding import PartitionSpec as P

BROWS = 128
TILE = 64
DST = 128
SIDE = 4
CHIPS = SIDE**3
AXES = ("shard", "basis")
CORE_SWAP = [(0, 1), (1, 0)]
CHUNKS = (((2, 0), (2, 1)), ((1, 0), (3, 0)), ((1, 1), (3, 1)), ((0, 0), (0, 1)))
FROM_BELOW, FROM_ABOVE = 1, 2
BF16 = jnp.bfloat16
F32 = jnp.float32
SMALL = pl.CostEstimate(flops=1, bytes_accessed=1, transcendentals=0)
VMEM_SMALL = 2 * 1024 * 1024
VMEM_LIMIT = 16 * 1024 * 1024


def device_id(x, y, z, core):
    return ((z % SIDE * SIDE + y % SIDE) * SIDE + x % SIDE) * 2 + core


def pairs(target):
    found = []
    for z in range(SIDE):
        for y in range(SIDE):
            for x in range(SIDE):
                for core in range(2):
                    found.append((device_id(x, y, z, core), device_id(*target(x, y, z, core))))
    assert len({to for _, to in found}) == len(found)
    return found


def hop1_pairs(step):
    return pairs(lambda x, y, z, core: (x + step, y, z, 0) if core == 0 else (x, y + step, z, 1))


def hop2_pairs(step):
    return pairs(lambda x, y, z, core: (x, y, z + step, core))


MATCHED = ((0, 0), (2, 1), (2, 0), (0, 1))
UNMATCHED = ((1, 1), (1, 0), (3, 1), (3, 0))


def hop3_pairs(send):
    def target(x, y, z, core):
        step, half = (MATCHED if (x + y + z) % 2 == core else UNMATCHED)[send]
        return (x, y + step, z, half) if core == 0 else (x + step, y, z, half)

    return pairs(target)


def coordinates():
    chip = lax.axis_index("shard")
    return chip % SIDE, chip // SIDE % SIDE, chip // (SIDE * SIDE), lax.axis_index("basis")


def group_of(x, y, z, kind, which):
    y_end = 2 * which + (x + z) % 2
    x_end = 2 * which + (y + z + 1) % 2
    return jnp.where(kind == 0, (z * SIDE + y_end) * SIDE + x, (z * SIDE + y) * SIDE + x_end)


def in_hbm(array):
    return pltpu.with_memory_space_constraint(array, pltpu.HBM)


def in_vmem(array):
    return pltpu.with_memory_space_constraint(array, pltpu.VMEM)


SMEM_SPEC = pl.BlockSpec(memory_space=pltpu.SMEM)
HBM_SPEC = pl.BlockSpec(memory_space=pltpu.HBM)
VMEM_SPEC = pl.BlockSpec(memory_space=pltpu.VMEM)


def notes_kernel(blocks, *refs):
    given, out_ref, held, sems = refs[:4], refs[4], refs[5:9], refs[9]
    copies = [pltpu.make_async_copy(a, b, sems.at[i]) for i, (a, b) in enumerate(zip(given, held))]
    for copy in copies:
        copy.start()
    for copy in copies:
        copy.wait()
    counts_ref, dests_ref, rels_ref, lists_ref = held
    rows = CHIPS * 8
    x, y, z, _ = coordinates()
    counts = counts_ref[...]
    before = (
        lax.broadcasted_iota(jnp.int32, (CHIPS, CHIPS), 0)
        < lax.broadcasted_iota(jnp.int32, (CHIPS, CHIPS), 1)
    ).astype(F32)
    used = jnp.broadcast_to(counts.astype(F32), (8, CHIPS))
    rank = jnp.dot(used, before, preferred_element_type=F32)[:1]
    where = jnp.where(counts > 0, rank, -1.0).astype(jnp.int32)
    row = lax.broadcasted_iota(jnp.int32, (rows, 1), 0)
    slot, place = row // 8, row % 8
    line = place % SIDE
    owner = jnp.where(
        (x + y + z) % 2 == 0,
        slot // SIDE * SIDE + line,
        slot // 16 * 16 + line * SIDE + slot % SIDE,
    )

    def lookup(values, index):
        lane = lax.broadcasted_iota(jnp.int32, (rows, values.shape[1]), 1)
        return jnp.sum(jnp.where(lane == index, values, 0), axis=1, keepdims=True)

    position = lookup(where, owner)
    hit = (position == lax.broadcasted_iota(jnp.int32, (rows, blocks), 1)).astype(BF16)
    dests = jnp.concatenate([dests_ref[:, p * BROWS : (p + 1) * BROWS] for p in range(blocks)], axis=0)
    dests = jnp.dot(hit, dests.astype(BF16), preferred_element_type=F32).astype(jnp.int32)
    codes = jnp.where(position < 0, -1, dests + jnp.where(position >= blocks // 2, DST, 0))
    block = lookup(jnp.where(counts > 0, lists_ref[...], -1), slot)
    lane = lax.broadcasted_iota(jnp.int32, (rows, DST), 1)
    other = jnp.where(lane == 0, codes, block)
    for tile in range(BROWS // TILE):
        rel = lookup(rels_ref[...], position * (BROWS // TILE) + tile)
        other = jnp.where(lane == 1 + tile, rel, other)
    out_ref[...] = jnp.where(place < SIDE, codes, other)


def make_notes(*given):
    return pl.pallas_call(
        functools.partial(notes_kernel, given[1].shape[1] // BROWS),
        out_shape=jax.ShapeDtypeStruct((CHIPS * 8, DST), jnp.int32),
        in_specs=[HBM_SPEC] * 4,
        out_specs=VMEM_SPEC,
        scratch_shapes=[pltpu.VMEM(array.shape, jnp.int32) for array in given] + [pltpu.SemaphoreType.DMA((4,))],
        compiler_params=pltpu.CompilerParams(vmem_limit_bytes=VMEM_LIMIT),
        name="notes",
    )(*map(in_hbm, given)).reshape(CHIPS, 8, DST)


WORDS = 4
HOP1 = (1, 3, 2)


def word(words_ref, group, line, which):
    return words_ref[(group * SIDE + line) * WORDS + which]


def reached(step, kind, step_z, which):
    x, y, z, _ = coordinates()
    x_to = jnp.where(kind == 0, (x + step) % SIDE, x)
    y_to = jnp.where(kind == 0, y, (y + step) % SIDE)
    return group_of(x_to, y_to, (z + step_z) % SIDE, kind, which)


def local_block(words_ref, table_ref, group):
    block = word(words_ref, group, 0, WORDS - 1)
    start = pl.multiple_of(jnp.maximum(block, 0) * BROWS, BROWS)
    return block >= 0, table_ref.at[pl.ds(start, BROWS)]


def run_moves(moves):
    for live, copies in moves:

        @pl.when(live)
        def _(copies=copies):
            for copy in copies:
                copy.start()

    for live, copies in moves:

        @pl.when(live)
        def _(copies=copies):
            for copy in copies:
                copy.wait()


def cross_kernel(chunks, words_ref, table_ref, out_ref, sems):
    core = lax.axis_index("basis")
    moves = []
    for i, chunk in enumerate(chunks):
        for step in range(SIDE):
            for pair, place in enumerate(chunk):
                live, source = local_block(words_ref, table_ref, reached(step, 1 - core, *place))
                at = (i, step, pair)
                moves.append((live, (pltpu.make_async_copy(source, out_ref.at[at], sems.at[at]),)))
    run_moves(moves)


def cross(chunks, words, table):
    shape = (len(chunks), SIDE, 2, BROWS, table.shape[1])
    return pl.pallas_call(
        functools.partial(cross_kernel, chunks),
        out_shape=pltpu.VMEM(shape, BF16),
        in_specs=[SMEM_SPEC, HBM_SPEC],
        out_specs=VMEM_SPEC,
        scratch_shapes=[pltpu.SemaphoreType.DMA((len(chunks), SIDE, 2))],
        compiler_params=pltpu.CompilerParams(vmem_limit_bytes=VMEM_SMALL),
        cost_estimate=SMALL,
        name="cross",
    )(words, in_hbm(table))


def pick_kernel(chunk, row, words_ref, table_ref, crossed_ref, *rest):
    outs, sems = rest[: len(HOP1)], rest[len(HOP1)]
    core = lax.axis_index("basis")
    moves = []
    for j, step in enumerate(HOP1):
        for pair, place in enumerate(chunk):
            live, source = local_block(words_ref, table_ref, reached(step, core, *place))
            copies = (
                pltpu.make_async_copy(source, outs[j].at[pair, 0], sems.at[0, j, pair]),
                pltpu.make_async_copy(crossed_ref.at[row, step, pair], outs[j].at[pair, 1], sems.at[1, j, pair]),
            )
            moves.append((live, copies))
    run_moves(moves)


def pick(chunk, row, words, table, crossed):
    return pl.pallas_call(
        functools.partial(pick_kernel, chunk, row),
        out_shape=[pltpu.VMEM((2, 2, BROWS, table.shape[1]), BF16)] * len(HOP1),
        in_specs=[SMEM_SPEC, HBM_SPEC, VMEM_SPEC],
        out_specs=[VMEM_SPEC] * len(HOP1),
        scratch_shapes=[pltpu.SemaphoreType.DMA((2, len(HOP1), 2))],
        compiler_params=pltpu.CompilerParams(vmem_limit_bytes=VMEM_SMALL),
        cost_estimate=SMALL,
        name="pick",
    )(words, in_hbm(table), in_vmem(crossed))


def project_kernel(chunk, row, added, words_ref, table_ref, own_basis, other_basis, notes_ref, coeffs_ref, crossed_ref, *rest):
    received, rest = rest[: len(HOP1)], rest[len(HOP1) :]
    extra, rest = rest[: len(added)], rest[len(added) :]
    outs, (local, total, sems) = rest[:2], rest[2:]
    x, y, z, core = coordinates()
    width = table_ref.shape[1]
    along = jnp.where(core == 0, x, y)
    pieces = []
    for which, place in enumerate(chunk):
        group = reached(0, core, *place)
        for step in HOP1 + (0,):
            line = (along - step) % SIDE
            code = word(words_ref, group, line, 0)
            rels = [word(words_ref, group, line, 1 + tile) for tile in range(2)]
            copy = None
            if step == 0:
                copy = pltpu.make_async_copy(
                    local_block(words_ref, table_ref, group)[1], local.at[which], sems.at[which]
                )
                pl.when(code >= 0)(copy.start)
            pieces.append((which, step, group, line, code, rels, copy))
    total[...] = jnp.zeros_like(total)
    lane = lax.broadcasted_iota(jnp.int32, (2, BROWS), 1)
    dest = lax.broadcasted_iota(jnp.int32, (DST, BROWS), 0)
    for which, step, group, line, code, rels, copy in pieces:

        @pl.when(code >= 0)
        def _(which=which, step=step, group=group, line=line, code=code, rels=rels, copy=copy):
            half = jnp.where(code >= DST, 1, 0)
            hit = notes_ref[group, pl.ds(line, 1), :] - half * DST == dest
            coef = [
                jnp.sum(
                    jnp.where(lane == rels[tile] % DST, coeffs_ref[rels[tile] // DST], 0.0), axis=1, keepdims=True
                )
                for tile in range(2)
            ]
            weights = jnp.where(lane < TILE, coef[0], coef[1])
            chosen = []
            for k in range(2):
                weight = jnp.where(core == 0, weights[k : k + 1], weights[1 - k : 2 - k])
                high = weight.astype(BF16).astype(F32)
                high, low = jnp.where(hit, high, 0.0), jnp.where(hit, weight - high, 0.0)
                chosen.append(jnp.concatenate([high, low], axis=1))
            chosen = jnp.concatenate(chosen, axis=0).astype(BF16)
            for part in range(2):
                if step > 0:
                    block = received[HOP1.index(step)][which, part]
                elif part == 1:
                    block = crossed_ref[row, 0, which]
                else:
                    copy.wait()
                    block = local[which]
                sums = jnp.dot(chosen, jnp.concatenate([block, block], axis=0), preferred_element_type=F32)
                column = pl.multiple_of(jnp.where(core == part, 0, width), width)
                total[which, half, :, pl.ds(column, width)] += sums

    summed = [
        total[:, :, k * DST : (k + 1) * DST, :].reshape(4 * DST, 2 * width).astype(BF16) for k in range(2)
    ]
    wide = own_basis.shape[1]
    tile = 256
    for start in range(0, wide, tile):
        result = jnp.dot(summed[0], own_basis[:, start : start + tile], preferred_element_type=F32)
        result += jnp.dot(summed[1], other_basis[:, start : start + tile], preferred_element_type=F32)
        result = result.reshape(2, 2, DST, tile)
        for which in range(2):
            here = result[which]
            if which in added:
                here += extra[added.index(which)][:, :, start : start + tile].astype(F32)
            outs[which][:, :, start : start + tile] = here.astype(outs[which].dtype)


def project(chunk, row, added, kept, words, table, *others):
    width = table.shape[1]
    wide = 2 * width
    return pl.pallas_call(
        functools.partial(project_kernel, chunk, row, added),
        out_shape=[pltpu.VMEM((2, DST, wide), F32 if which in kept else BF16) for which in range(2)],
        in_specs=[SMEM_SPEC, HBM_SPEC] + [VMEM_SPEC] * len(others),
        out_specs=[VMEM_SPEC] * 2,
        scratch_shapes=[
            pltpu.VMEM((2, BROWS, width), BF16),
            pltpu.VMEM((2, 2, 2 * DST, 2 * width), F32),
            pltpu.SemaphoreType.DMA((2,)),
        ],
        cost_estimate=pl.CostEstimate(flops=6 * 10**9, bytes_accessed=20 * 10**6, transcendentals=0),
        compiler_params=pltpu.CompilerParams(vmem_limit_bytes=VMEM_LIMIT),
        name="project",
    )(words, in_hbm(table), *map(in_vmem, others))


def join_kernel(part_ref, relayed_ref, out_ref):
    out_ref[...] = (part_ref[...] + relayed_ref[...].astype(F32)).astype(BF16)


def join(part, relayed):
    return pl.pallas_call(
        join_kernel,
        out_shape=pltpu.VMEM(part.shape, BF16),
        in_specs=[VMEM_SPEC] * 2,
        out_specs=VMEM_SPEC,
        compiler_params=pltpu.CompilerParams(vmem_limit_bytes=VMEM_SMALL),
        cost_estimate=SMALL,
        name="join",
    )(in_vmem(part), in_vmem(relayed))


def merge_kernel(*refs):
    ins, outs = refs[:6], refs[6:]
    x, y, z, core = coordinates()
    last = jnp.where(core == 0, y, x)
    matched = (x + y + z) % 2 == core
    for send, ((step, to), (other_step, other_to)) in enumerate(zip(MATCHED, UNMATCHED)):
        which = (last + jnp.where(matched, step, other_step)) % SIDE // 2
        half = jnp.where(matched, to, other_to)
        for group in range(2):

            @pl.when(which == group)
            def _(group=group, half=half, send=send):
                result = ins[3 * group][half].astype(F32)
                for other in ins[3 * group + 1 : 3 * group + 3]:
                    result += other[half].astype(F32)
                outs[send][...] = result.astype(BF16)


def merge(parts):
    return pl.pallas_call(
        merge_kernel,
        out_shape=[pltpu.VMEM(parts[0].shape[1:], BF16)] * 4,
        in_specs=[VMEM_SPEC] * len(parts),
        out_specs=[VMEM_SPEC] * 4,
        compiler_params=pltpu.CompilerParams(vmem_limit_bytes=VMEM_LIMIT),
        cost_estimate=SMALL,
        name="merge",
    )(*map(in_vmem, parts))


def degree_kernel(dests_ref, out_ref):
    rows = dests_ref.shape[1] // 2
    mine = dests_ref[:, pl.ds(pl.multiple_of(lax.axis_index("basis") * rows, BROWS), rows)]
    hit = mine == lax.broadcasted_iota(jnp.int32, (DST, rows), 0)
    count = jnp.sum(jnp.where(hit, 1.0, 0.0), axis=1, keepdims=True)
    out_ref[...] = jnp.broadcast_to(jnp.maximum(count, 1.0), out_ref.shape)


def degrees(dests):
    return pl.pallas_call(
        degree_kernel,
        out_shape=pltpu.VMEM((DST, BROWS), F32),
        in_specs=[VMEM_SPEC],
        out_specs=VMEM_SPEC,
        compiler_params=pltpu.CompilerParams(vmem_limit_bytes=2 * VMEM_SMALL),
        cost_estimate=SMALL,
        name="degree",
    )(dests)


def table_kernel(coeffs_ref, out_ref):
    rels = coeffs_ref.shape[1]
    for i in range(out_ref.shape[0]):
        here = min(DST, rels - i * DST)
        out_ref[i, :, :here] = coeffs_ref[:, i * DST : i * DST + here]


def make_table(coeffs):
    rels = coeffs.shape[0]
    return pl.pallas_call(
        table_kernel,
        out_shape=pltpu.VMEM((-(-rels // DST), 2, DST), F32),
        in_specs=[VMEM_SPEC],
        out_specs=VMEM_SPEC,
        compiler_params=pltpu.CompilerParams(vmem_limit_bytes=2 * VMEM_SMALL),
        cost_estimate=SMALL,
        name="table",
    )(coeffs.T)


def finish_kernel(degree_ref, *refs):
    ends, out_ref = refs[:-1], refs[-1]
    degree = degree_ref[...]
    for start in range(0, out_ref.shape[1], BROWS):
        here = slice(start, start + BROWS)
        summed = ends[0][:, here].astype(F32)
        for end in ends[1:]:
            summed += end[:, here].astype(F32)
        out_ref[:, here] = (summed / degree).astype(BF16)


def finish(degree, ends):
    return pl.pallas_call(
        finish_kernel,
        out_shape=jax.ShapeDtypeStruct(ends[0].shape, BF16),
        in_specs=[VMEM_SPEC] * (1 + len(ends)),
        out_specs=VMEM_SPEC,
        compiler_params=pltpu.CompilerParams(vmem_limit_bytes=2 * VMEM_SMALL),
        cost_estimate=SMALL,
        name="finish",
    )(*map(in_vmem, (degree, *ends)))


def body(features, bases, coeffs, block_lists, block_counts, tile_rel, dest_ids):
    other_basis = lax.ppermute(bases[0], "basis", CORE_SWAP)

    sent = make_notes(block_counts, dest_ids, tile_rel, block_lists.reshape(1, CHIPS))
    notes = lax.all_to_all(sent, "shard", split_axis=0, concat_axis=0, tiled=True)
    words = notes[:, SIDE:, :WORDS].reshape(-1)
    table, degree = make_table(coeffs), degrees(dest_ids)

    words, other_basis = lax.optimization_barrier((words, other_basis))
    both = bases[0], other_basis

    first = cross(CHUNKS[:1], words, features)
    first, later = lax.optimization_barrier((first, words))
    second = cross(CHUNKS[1:], later, features)
    first = lax.ppermute(first, "basis", CORE_SWAP)
    first, second = lax.optimization_barrier((first, second))
    second = lax.ppermute(second, "basis", CORE_SWAP)
    crossed = [(0, first)] + [(i, second) for i in range(len(CHUNKS) - 1)]

    def pick_chunk(i, after):
        (row, buf), (ready, _) = crossed[i], lax.optimization_barrier((words, after))
        bufs = pick(CHUNKS[i], row, ready, features, buf)
        return lax.optimization_barrier((bufs, words))

    picked, ready = [pick_chunk(0, words)[0]], words
    bufs, ready = pick_chunk(1, picked[0])
    picked.append(bufs)
    arrived, parts = [], []
    for i, (chunk, (row, buf)) in enumerate(zip(CHUNKS, crossed)):
        came = []
        for j, step in enumerate(HOP1):
            sent = picked[i][j]
            if i > 1:
                sent, arrived[-2][j] = lax.optimization_barrier((sent, arrived[-2][j]))
            came.append(lax.ppermute(sent, AXES, hop1_pairs(step)))
        arrived.append(came)
        given = [ready, features, *both, notes, table, buf, *came]
        added = ()
        if i == FROM_ABOVE:
            added, given = (1,), given + [parts[0][1]]
        part = project(chunk, row, added, (0,) if i == FROM_BELOW else (), *given)
        if i + 2 < len(CHUNKS):
            bufs, ready = pick_chunk(i + 2, part)
            picked.append(bufs)
        if i == FROM_BELOW:
            part = [join(part[0], parts[0][0]), part[1]]
            part[0], parts[0][1] = lax.optimization_barrier((part[0], parts[0][1]))
        if i == FROM_ABOVE:
            part, parts[-1] = lax.optimization_barrier((part, parts[-1]))
        if i < len(CHUNKS) - 1:
            part = [lax.ppermute(p, AXES, hop2_pairs(step)) for p, step in zip(part, (1, 3))]
        parts.append(part)
    parts = [parts[3][0], *parts[1], parts[3][1], *parts[2]]

    merged = merge(parts)
    ends = [lax.ppermute(buf, AXES, hop3_pairs(send)) for send, buf in enumerate(merged)]
    return finish(degree, ends)


def solution(mesh):
    placed = (
        P("shard", "basis"),
        P("basis", None, None),
        P(),
        P("shard", None, None),
        P("shard", None),
        P("shard", None),
        P("shard", None),
    )
    return jax.shard_map(
        body, mesh=mesh, in_specs=placed, out_specs=P(("shard", "basis"), None), check_vma=False
    )
```

```python
import functools

import jax
import jax.numpy as jnp
from jax import lax
from jax.experimental import pallas as pl
from jax.experimental.pallas import tpu as pltpu
from jax.sharding import PartitionSpec as P

BROWS = 128
TILE = 64
DST = 128
SIDE = 4
CHIPS = SIDE**3
AXES = ("shard", "basis")
CORE_SWAP = [(0, 1), (1, 0)]
CHUNKS = (((2, 0), (2, 1)), ((1, 0), (3, 0)), ((1, 1), (3, 1)), ((0, 0), (0, 1)))
FROM_BELOW, FROM_ABOVE = 1, 2
BF16 = jnp.bfloat16
F32 = jnp.float32
SMALL = pl.CostEstimate(flops=1, bytes_accessed=1, transcendentals=0)
VMEM_SMALL = 2 * 1024 * 1024
VMEM_LIMIT = 16 * 1024 * 1024


def device_id(x, y, z, core):
    return ((z % SIDE * SIDE + y % SIDE) * SIDE + x % SIDE) * 2 + core


def pairs(target):
    found = []
    for z in range(SIDE):
        for y in range(SIDE):
            for x in range(SIDE):
                for core in range(2):
                    found.append((device_id(x, y, z, core), device_id(*target(x, y, z, core))))
    assert len({to for _, to in found}) == len(found)
    return found


def hop1_pairs(step):
    return pairs(lambda x, y, z, core: (x + step, y, z, 0) if core == 0 else (x, y + step, z, 1))


def hop2_pairs(step):
    return pairs(lambda x, y, z, core: (x, y, z + step, core))


MATCHED = ((2, 1), (2, 0), (0, 0), (0, 1))
UNMATCHED = ((1, 0), (3, 1), (1, 1), (3, 0))


def hop3_pairs(send):
    def target(x, y, z, core):
        step, half = (MATCHED if (x + y + z) % 2 == core else UNMATCHED)[send]
        return (x, y + step, z, half) if core == 0 else (x + step, y, z, half)

    return pairs(target)


def coordinates():
    chip = lax.axis_index("shard")
    return chip % SIDE, chip // SIDE % SIDE, chip // (SIDE * SIDE), lax.axis_index("basis")


def group_of(x, y, z, kind, which):
    y_end = 2 * which + (x + z) % 2
    x_end = 2 * which + (y + z + 1) % 2
    return jnp.where(kind == 0, (z * SIDE + y_end) * SIDE + x, (z * SIDE + y) * SIDE + x_end)


def in_hbm(array):
    return pltpu.with_memory_space_constraint(array, pltpu.HBM)


def in_vmem(array):
    return pltpu.with_memory_space_constraint(array, pltpu.VMEM)


SMEM_SPEC = pl.BlockSpec(memory_space=pltpu.SMEM)
HBM_SPEC = pl.BlockSpec(memory_space=pltpu.HBM)
VMEM_SPEC = pl.BlockSpec(memory_space=pltpu.VMEM)


def notes_kernel(blocks, *refs):
    given, out_ref, held, sems = refs[:4], refs[4], refs[5:9], refs[9]
    copies = [pltpu.make_async_copy(a, b, sems.at[i]) for i, (a, b) in enumerate(zip(given, held))]
    for copy in copies:
        copy.start()
    for copy in copies:
        copy.wait()
    counts_ref, dests_ref, rels_ref, lists_ref = held
    rows = CHIPS * 8
    x, y, z, _ = coordinates()
    counts = counts_ref[...]
    before = (
        lax.broadcasted_iota(jnp.int32, (CHIPS, CHIPS), 0)
        < lax.broadcasted_iota(jnp.int32, (CHIPS, CHIPS), 1)
    ).astype(F32)
    used = jnp.broadcast_to(counts.astype(F32), (8, CHIPS))
    rank = jnp.dot(used, before, preferred_element_type=F32)[:1]
    where = jnp.where(counts > 0, rank, -1.0).astype(jnp.int32)
    row = lax.broadcasted_iota(jnp.int32, (rows, 1), 0)
    slot, place = row // 8, row % 8
    line = place % SIDE
    owner = jnp.where(
        (x + y + z) % 2 == 0,
        slot // SIDE * SIDE + line,
        slot // 16 * 16 + line * SIDE + slot % SIDE,
    )

    def lookup(values, index):
        lane = lax.broadcasted_iota(jnp.int32, (rows, values.shape[1]), 1)
        return jnp.sum(jnp.where(lane == index, values, 0), axis=1, keepdims=True)

    position = lookup(where, owner)
    hit = (position == lax.broadcasted_iota(jnp.int32, (rows, blocks), 1)).astype(BF16)
    dests = jnp.concatenate([dests_ref[:, p * BROWS : (p + 1) * BROWS] for p in range(blocks)], axis=0)
    dests = jnp.dot(hit, dests.astype(BF16), preferred_element_type=F32).astype(jnp.int32)
    codes = jnp.where(position < 0, -1, dests + jnp.where(position >= blocks // 2, DST, 0))
    block = lookup(jnp.where(counts > 0, lists_ref[...], -1), slot)
    lane = lax.broadcasted_iota(jnp.int32, (rows, DST), 1)
    other = jnp.where(lane == 0, codes, block)
    for tile in range(BROWS // TILE):
        rel = lookup(rels_ref[...], position * (BROWS // TILE) + tile)
        other = jnp.where(lane == 1 + tile, rel, other)
    out_ref[...] = jnp.where(place < SIDE, codes, other)


def make_notes(*given):
    return pl.pallas_call(
        functools.partial(notes_kernel, given[1].shape[1] // BROWS),
        out_shape=jax.ShapeDtypeStruct((CHIPS * 8, DST), jnp.int32),
        in_specs=[HBM_SPEC] * 4,
        out_specs=VMEM_SPEC,
        scratch_shapes=[pltpu.VMEM(array.shape, jnp.int32) for array in given] + [pltpu.SemaphoreType.DMA((4,))],
        compiler_params=pltpu.CompilerParams(vmem_limit_bytes=VMEM_LIMIT),
        name="notes",
    )(*map(in_hbm, given)).reshape(CHIPS, 8, DST)


WORDS = 4
HOP1 = (1, 3, 2)


def word(words_ref, group, line, which):
    return words_ref[(group * SIDE + line) * WORDS + which]


def reached(step, kind, step_z, which):
    x, y, z, _ = coordinates()
    x_to = jnp.where(kind == 0, (x + step) % SIDE, x)
    y_to = jnp.where(kind == 0, y, (y + step) % SIDE)
    return group_of(x_to, y_to, (z + step_z) % SIDE, kind, which)


def local_block(words_ref, table_ref, group):
    block = word(words_ref, group, 0, WORDS - 1)
    start = pl.multiple_of(jnp.maximum(block, 0) * BROWS, BROWS)
    return block >= 0, table_ref.at[pl.ds(start, BROWS)]


def run_moves(moves):
    for live, copies in moves:

        @pl.when(live)
        def _(copies=copies):
            for copy in copies:
                copy.start()

    for live, copies in moves:

        @pl.when(live)
        def _(copies=copies):
            for copy in copies:
                copy.wait()


def cross_kernel(chunks, words_ref, table_ref, out_ref, sems):
    core = lax.axis_index("basis")
    moves = []
    for i, chunk in enumerate(chunks):
        for step in range(SIDE):
            for pair, place in enumerate(chunk):
                live, source = local_block(words_ref, table_ref, reached(step, 1 - core, *place))
                at = (i, step, pair)
                moves.append((live, (pltpu.make_async_copy(source, out_ref.at[at], sems.at[at]),)))
    run_moves(moves)


def cross(chunks, words, table):
    shape = (len(chunks), SIDE, 2, BROWS, table.shape[1])
    return pl.pallas_call(
        functools.partial(cross_kernel, chunks),
        out_shape=pltpu.VMEM(shape, BF16),
        in_specs=[SMEM_SPEC, HBM_SPEC],
        out_specs=VMEM_SPEC,
        scratch_shapes=[pltpu.SemaphoreType.DMA((len(chunks), SIDE, 2))],
        compiler_params=pltpu.CompilerParams(vmem_limit_bytes=VMEM_SMALL),
        cost_estimate=SMALL,
        name="cross",
    )(words, in_hbm(table))


def pick_kernel(chunk, row, words_ref, table_ref, crossed_ref, *rest):
    outs, sems = rest[: len(HOP1)], rest[len(HOP1)]
    core = lax.axis_index("basis")
    moves = []
    for j, step in enumerate(HOP1):
        for pair, place in enumerate(chunk):
            live, source = local_block(words_ref, table_ref, reached(step, core, *place))
            copies = (
                pltpu.make_async_copy(source, outs[j].at[pair, 0], sems.at[0, j, pair]),
                pltpu.make_async_copy(crossed_ref.at[row, step, pair], outs[j].at[pair, 1], sems.at[1, j, pair]),
            )
            moves.append((live, copies))
    run_moves(moves)


def pick(chunk, row, words, table, crossed):
    return pl.pallas_call(
        functools.partial(pick_kernel, chunk, row),
        out_shape=[pltpu.VMEM((2, 2, BROWS, table.shape[1]), BF16)] * len(HOP1),
        in_specs=[SMEM_SPEC, HBM_SPEC, VMEM_SPEC],
        out_specs=[VMEM_SPEC] * len(HOP1),
        scratch_shapes=[pltpu.SemaphoreType.DMA((2, len(HOP1), 2))],
        compiler_params=pltpu.CompilerParams(vmem_limit_bytes=VMEM_SMALL),
        cost_estimate=SMALL,
        name="pick",
    )(words, in_hbm(table), in_vmem(crossed))


def project_kernel(chunk, row, added, words_ref, table_ref, own_basis, other_basis, notes_ref, coeffs_ref, crossed_ref, *rest):
    received, rest = rest[: len(HOP1)], rest[len(HOP1) :]
    extra, rest = rest[: len(added)], rest[len(added) :]
    outs, (local, total, sems) = rest[:2], rest[2:]
    x, y, z, core = coordinates()
    width = table_ref.shape[1]
    along = jnp.where(core == 0, x, y)
    pieces = []
    for which, place in enumerate(chunk):
        group = reached(0, core, *place)
        for step in HOP1 + (0,):
            line = (along - step) % SIDE
            code = word(words_ref, group, line, 0)
            rels = [word(words_ref, group, line, 1 + tile) for tile in range(2)]
            copy = None
            if step == 0:
                copy = pltpu.make_async_copy(
                    local_block(words_ref, table_ref, group)[1], local.at[which], sems.at[which]
                )
                pl.when(code >= 0)(copy.start)
            pieces.append((which, step, group, line, code, rels, copy))
    total[...] = jnp.zeros_like(total)
    lane = lax.broadcasted_iota(jnp.int32, (2, BROWS), 1)
    dest = lax.broadcasted_iota(jnp.int32, (DST, BROWS), 0)
    for which, step, group, line, code, rels, copy in pieces:

        @pl.when(code >= 0)
        def _(which=which, step=step, group=group, line=line, code=code, rels=rels, copy=copy):
            half = jnp.where(code >= DST, 1, 0)
            hit = notes_ref[group, pl.ds(line, 1), :] - half * DST == dest
            coef = [
                jnp.sum(
                    jnp.where(lane == rels[tile] % DST, coeffs_ref[rels[tile] // DST], 0.0), axis=1, keepdims=True
                )
                for tile in range(2)
            ]
            weights = jnp.where(lane < TILE, coef[0], coef[1])
            chosen = []
            for k in range(2):
                weight = jnp.where(core == 0, weights[k : k + 1], weights[1 - k : 2 - k])
                high = weight.astype(BF16).astype(F32)
                high, low = jnp.where(hit, high, 0.0), jnp.where(hit, weight - high, 0.0)
                chosen.append(jnp.concatenate([high, low], axis=1))
            chosen = jnp.concatenate(chosen, axis=0).astype(BF16)
            for part in range(2):
                if step > 0:
                    block = received[HOP1.index(step)][which, part]
                elif part == 1:
                    block = crossed_ref[row, 0, which]
                else:
                    copy.wait()
                    block = local[which]
                sums = jnp.dot(chosen, jnp.concatenate([block, block], axis=0), preferred_element_type=F32)
                column = pl.multiple_of(jnp.where(core == part, 0, width), width)
                total[which, half, :, pl.ds(column, width)] += sums

    summed = [
        total[:, :, k * DST : (k + 1) * DST, :].reshape(4 * DST, 2 * width).astype(BF16) for k in range(2)
    ]
    wide = own_basis.shape[1]
    tile = 256
    for start in range(0, wide, tile):
        result = jnp.dot(summed[0], own_basis[:, start : start + tile], preferred_element_type=F32)
        result += jnp.dot(summed[1], other_basis[:, start : start + tile], preferred_element_type=F32)
        result = result.reshape(2, 2, DST, tile)
        for which in range(2):
            here = result[which]
            if which in added:
                here += extra[added.index(which)][:, :, start : start + tile].astype(F32)
            outs[which][:, :, start : start + tile] = here.astype(outs[which].dtype)


def project(chunk, row, added, kept, words, table, *others):
    width = table.shape[1]
    wide = 2 * width
    return pl.pallas_call(
        functools.partial(project_kernel, chunk, row, added),
        out_shape=[pltpu.VMEM((2, DST, wide), F32 if which in kept else BF16) for which in range(2)],
        in_specs=[SMEM_SPEC, HBM_SPEC] + [VMEM_SPEC] * len(others),
        out_specs=[VMEM_SPEC] * 2,
        scratch_shapes=[
            pltpu.VMEM((2, BROWS, width), BF16),
            pltpu.VMEM((2, 2, 2 * DST, 2 * width), F32),
            pltpu.SemaphoreType.DMA((2,)),
        ],
        cost_estimate=pl.CostEstimate(flops=6 * 10**9, bytes_accessed=20 * 10**6, transcendentals=0),
        compiler_params=pltpu.CompilerParams(vmem_limit_bytes=VMEM_LIMIT),
        name="project",
    )(words, in_hbm(table), *map(in_vmem, others))


def join_kernel(part_ref, relayed_ref, out_ref):
    out_ref[...] = (part_ref[...] + relayed_ref[...].astype(F32)).astype(BF16)


def join(part, relayed):
    return pl.pallas_call(
        join_kernel,
        out_shape=pltpu.VMEM(part.shape, BF16),
        in_specs=[VMEM_SPEC] * 2,
        out_specs=VMEM_SPEC,
        compiler_params=pltpu.CompilerParams(vmem_limit_bytes=VMEM_SMALL),
        cost_estimate=SMALL,
        name="join",
    )(in_vmem(part), in_vmem(relayed))


def merge_kernel(*refs):
    ins, outs = refs[:6], refs[6:]
    x, y, z, core = coordinates()
    last = jnp.where(core == 0, y, x)
    matched = (x + y + z) % 2 == core
    for send, ((step, to), (other_step, other_to)) in enumerate(zip(MATCHED, UNMATCHED)):
        which = (last + jnp.where(matched, step, other_step)) % SIDE // 2
        half = jnp.where(matched, to, other_to)
        for group in range(2):

            @pl.when(which == group)
            def _(group=group, half=half, send=send):
                result = ins[3 * group][half].astype(F32)
                for other in ins[3 * group + 1 : 3 * group + 3]:
                    result += other[half].astype(F32)
                outs[send][...] = result.astype(BF16)


def merge(parts):
    return pl.pallas_call(
        merge_kernel,
        out_shape=[pltpu.VMEM(parts[0].shape[1:], BF16)] * 4,
        in_specs=[VMEM_SPEC] * len(parts),
        out_specs=[VMEM_SPEC] * 4,
        compiler_params=pltpu.CompilerParams(vmem_limit_bytes=VMEM_LIMIT),
        cost_estimate=SMALL,
        name="merge",
    )(*map(in_vmem, parts))


def degree_kernel(dests_ref, out_ref):
    rows = dests_ref.shape[1] // 2
    mine = dests_ref[:, pl.ds(pl.multiple_of(lax.axis_index("basis") * rows, BROWS), rows)]
    hit = mine == lax.broadcasted_iota(jnp.int32, (DST, rows), 0)
    count = jnp.sum(jnp.where(hit, 1.0, 0.0), axis=1, keepdims=True)
    out_ref[...] = jnp.broadcast_to(jnp.maximum(count, 1.0), out_ref.shape)


def degrees(dests):
    return pl.pallas_call(
        degree_kernel,
        out_shape=pltpu.VMEM((DST, BROWS), F32),
        in_specs=[VMEM_SPEC],
        out_specs=VMEM_SPEC,
        compiler_params=pltpu.CompilerParams(vmem_limit_bytes=2 * VMEM_SMALL),
        cost_estimate=SMALL,
        name="degree",
    )(dests)


def table_kernel(coeffs_ref, out_ref):
    rels = coeffs_ref.shape[1]
    for i in range(out_ref.shape[0]):
        here = min(DST, rels - i * DST)
        out_ref[i, :, :here] = coeffs_ref[:, i * DST : i * DST + here]


def make_table(coeffs):
    rels = coeffs.shape[0]
    return pl.pallas_call(
        table_kernel,
        out_shape=pltpu.VMEM((-(-rels // DST), 2, DST), F32),
        in_specs=[VMEM_SPEC],
        out_specs=VMEM_SPEC,
        compiler_params=pltpu.CompilerParams(vmem_limit_bytes=2 * VMEM_SMALL),
        cost_estimate=SMALL,
        name="table",
    )(coeffs.T)


def finish_kernel(degree_ref, *refs):
    ends, out_ref = refs[:-1], refs[-1]
    degree = degree_ref[...]
    for start in range(0, out_ref.shape[1], BROWS):
        here = slice(start, start + BROWS)
        summed = ends[0][:, here].astype(F32)
        for end in ends[1:]:
            summed += end[:, here].astype(F32)
        out_ref[:, here] = (summed / degree).astype(BF16)


def finish(degree, ends):
    return pl.pallas_call(
        finish_kernel,
        out_shape=jax.ShapeDtypeStruct(ends[0].shape, BF16),
        in_specs=[VMEM_SPEC] * (1 + len(ends)),
        out_specs=VMEM_SPEC,
        compiler_params=pltpu.CompilerParams(vmem_limit_bytes=2 * VMEM_SMALL),
        cost_estimate=SMALL,
        name="finish",
    )(*map(in_vmem, (degree, *ends)))


def body(features, bases, coeffs, block_lists, block_counts, tile_rel, dest_ids):
    other_basis = lax.ppermute(bases[0], "basis", CORE_SWAP)

    sent = make_notes(block_counts, dest_ids, tile_rel, block_lists.reshape(1, CHIPS))
    notes = lax.all_to_all(sent, "shard", split_axis=0, concat_axis=0, tiled=True)
    words = notes[:, SIDE:, :WORDS].reshape(-1)
    table, degree = make_table(coeffs), degrees(dest_ids)

    words, other_basis = lax.optimization_barrier((words, other_basis))
    both = bases[0], other_basis

    first = cross(CHUNKS[:1], words, features)
    first, later = lax.optimization_barrier((first, words))
    second = cross(CHUNKS[1:], later, features)
    first = lax.ppermute(first, "basis", CORE_SWAP)
    first, second = lax.optimization_barrier((first, second))
    second = lax.ppermute(second, "basis", CORE_SWAP)
    crossed = [(0, first)] + [(i, second) for i in range(len(CHUNKS) - 1)]

    def pick_chunk(i, after):
        (row, buf), (ready, _) = crossed[i], lax.optimization_barrier((words, after))
        bufs = pick(CHUNKS[i], row, ready, features, buf)
        return lax.optimization_barrier((bufs, words))

    picked, ready = [pick_chunk(0, words)[0]], words
    bufs, ready = pick_chunk(1, picked[0])
    picked.append(bufs)
    arrived, parts = [], []
    for i, (chunk, (row, buf)) in enumerate(zip(CHUNKS, crossed)):
        came = []
        for j, step in enumerate(HOP1):
            sent = picked[i][j]
            if i > 1:
                sent, arrived[-2][j] = lax.optimization_barrier((sent, arrived[-2][j]))
            came.append(lax.ppermute(sent, AXES, hop1_pairs(step)))
        arrived.append(came)
        given = [ready, features, *both, notes, table, buf, *came]
        added = ()
        if i == FROM_ABOVE:
            added, given = (1,), given + [parts[0][1]]
        part = project(chunk, row, added, (0,) if i == FROM_BELOW else (), *given)
        if i + 2 < len(CHUNKS):
            bufs, ready = pick_chunk(i + 2, part)
            picked.append(bufs)
        if i == FROM_BELOW:
            part = [join(part[0], parts[0][0]), part[1]]
            part[0], parts[0][1] = lax.optimization_barrier((part[0], parts[0][1]))
        if i == FROM_ABOVE:
            part, parts[-1] = lax.optimization_barrier((part, parts[-1]))
        if i < len(CHUNKS) - 1:
            part = [lax.ppermute(p, AXES, hop2_pairs(step)) for p, step in zip(part, (1, 3))]
        parts.append(part)
    parts = [parts[3][0], *parts[1], parts[3][1], *parts[2]]

    merged = merge(parts)
    ends = [lax.ppermute(buf, AXES, hop3_pairs(send)) for send, buf in enumerate(merged)]
    return finish(degree, ends)


def solution(mesh):
    placed = (
        P("shard", "basis"),
        P("basis", None, None),
        P(),
        P("shard", None, None),
        P("shard", None),
        P("shard", None),
        P("shard", None),
    )
    return jax.shard_map(
        body, mesh=mesh, in_specs=placed, out_specs=P(("shard", "basis"), None), check_vma=False
    )
```

```python
import functools

import jax
import jax.numpy as jnp
from jax import lax
from jax.experimental import pallas as pl
from jax.experimental.pallas import tpu as pltpu
from jax.sharding import PartitionSpec as P

BROWS = 128
TILE = 64
DST = 128
SIDE = 4
CHIPS = SIDE**3
AXES = ("shard", "basis")
CORE_SWAP = [(0, 1), (1, 0)]
CHUNKS = (((2, 0), (2, 1)), ((1, 0), (3, 0)), ((1, 1), (3, 1)), ((0, 0), (0, 1)))
FROM_BELOW, FROM_ABOVE = 1, 2
BF16 = jnp.bfloat16
F32 = jnp.float32
SMALL = pl.CostEstimate(flops=1, bytes_accessed=1, transcendentals=0)
VMEM_SMALL = 2 * 1024 * 1024
VMEM_LIMIT = 16 * 1024 * 1024


def device_id(x, y, z, core):
    return ((z % SIDE * SIDE + y % SIDE) * SIDE + x % SIDE) * 2 + core


def pairs(target):
    found = []
    for z in range(SIDE):
        for y in range(SIDE):
            for x in range(SIDE):
                for core in range(2):
                    found.append((device_id(x, y, z, core), device_id(*target(x, y, z, core))))
    assert len({to for _, to in found}) == len(found)
    return found


def hop1_pairs(step):
    return pairs(lambda x, y, z, core: (x + step, y, z, 0) if core == 0 else (x, y + step, z, 1))


def hop2_pairs(step):
    return pairs(lambda x, y, z, core: (x, y, z + step, core))


MATCHED = ((2, 1), (2, 0), (0, 0), (0, 1))
UNMATCHED = ((1, 0), (3, 1), (1, 1), (3, 0))


def hop3_pairs(send):
    def target(x, y, z, core):
        step, half = (MATCHED if (x + y + z) % 2 == core else UNMATCHED)[send]
        return (x, y + step, z, half) if core == 0 else (x + step, y, z, half)

    return pairs(target)


def coordinates():
    chip = lax.axis_index("shard")
    return chip % SIDE, chip // SIDE % SIDE, chip // (SIDE * SIDE), lax.axis_index("basis")


def group_of(x, y, z, kind, which):
    y_end = 2 * which + (x + z) % 2
    x_end = 2 * which + (y + z + 1) % 2
    return jnp.where(kind == 0, (z * SIDE + y_end) * SIDE + x, (z * SIDE + y) * SIDE + x_end)


def in_hbm(array):
    return pltpu.with_memory_space_constraint(array, pltpu.HBM)


def in_vmem(array):
    return pltpu.with_memory_space_constraint(array, pltpu.VMEM)


SMEM_SPEC = pl.BlockSpec(memory_space=pltpu.SMEM)
HBM_SPEC = pl.BlockSpec(memory_space=pltpu.HBM)
VMEM_SPEC = pl.BlockSpec(memory_space=pltpu.VMEM)


def notes_kernel(blocks, *refs):
    given, out_ref, held, sems = refs[:4], refs[4], refs[5:9], refs[9]
    copies = [pltpu.make_async_copy(a, b, sems.at[i]) for i, (a, b) in enumerate(zip(given, held))]
    for copy in copies:
        copy.start()
    for copy in copies:
        copy.wait()
    counts_ref, dests_ref, rels_ref, lists_ref = held
    rows = CHIPS * 8
    x, y, z, _ = coordinates()
    counts = counts_ref[...]
    before = (
        lax.broadcasted_iota(jnp.int32, (CHIPS, CHIPS), 0)
        < lax.broadcasted_iota(jnp.int32, (CHIPS, CHIPS), 1)
    ).astype(F32)
    used = jnp.broadcast_to(counts.astype(F32), (8, CHIPS))
    rank = jnp.dot(used, before, preferred_element_type=F32)[:1]
    where = jnp.where(counts > 0, rank, -1.0).astype(jnp.int32)
    row = lax.broadcasted_iota(jnp.int32, (rows, 1), 0)
    slot, place = row // 8, row % 8
    line = place % SIDE
    owner = jnp.where(
        (x + y + z) % 2 == 0,
        slot // SIDE * SIDE + line,
        slot // 16 * 16 + line * SIDE + slot % SIDE,
    )

    def lookup(values, index):
        lane = lax.broadcasted_iota(jnp.int32, (rows, values.shape[1]), 1)
        return jnp.sum(jnp.where(lane == index, values, 0), axis=1, keepdims=True)

    position = lookup(where, owner)
    hit = (position == lax.broadcasted_iota(jnp.int32, (rows, blocks), 1)).astype(BF16)
    dests = jnp.concatenate([dests_ref[:, p * BROWS : (p + 1) * BROWS] for p in range(blocks)], axis=0)
    dests = jnp.dot(hit, dests.astype(BF16), preferred_element_type=F32).astype(jnp.int32)
    codes = jnp.where(position < 0, -1, dests + jnp.where(position >= blocks // 2, DST, 0))
    block = lookup(jnp.where(counts > 0, lists_ref[...], -1), slot)
    lane = lax.broadcasted_iota(jnp.int32, (rows, DST), 1)
    other = jnp.where(lane == 0, codes, block)
    for tile in range(BROWS // TILE):
        rel = lookup(rels_ref[...], position * (BROWS // TILE) + tile)
        other = jnp.where(lane == 1 + tile, rel, other)
    out_ref[...] = jnp.where(place < SIDE, codes, other)


def make_notes(*given):
    return pl.pallas_call(
        functools.partial(notes_kernel, given[1].shape[1] // BROWS),
        out_shape=jax.ShapeDtypeStruct((CHIPS * 8, DST), jnp.int32),
        in_specs=[HBM_SPEC] * 4,
        out_specs=VMEM_SPEC,
        scratch_shapes=[pltpu.VMEM(array.shape, jnp.int32) for array in given] + [pltpu.SemaphoreType.DMA((4,))],
        compiler_params=pltpu.CompilerParams(vmem_limit_bytes=VMEM_LIMIT),
        name="notes",
    )(*map(in_hbm, given)).reshape(CHIPS, 8, DST)


WORDS = 4
HOP1 = (1, 3, 2)


def word(words_ref, group, line, which):
    return words_ref[(group * SIDE + line) * WORDS + which]


def reached(step, kind, step_z, which):
    x, y, z, _ = coordinates()
    x_to = jnp.where(kind == 0, (x + step) % SIDE, x)
    y_to = jnp.where(kind == 0, y, (y + step) % SIDE)
    return group_of(x_to, y_to, (z + step_z) % SIDE, kind, which)


def local_block(words_ref, table_ref, group):
    block = word(words_ref, group, 0, WORDS - 1)
    start = pl.multiple_of(jnp.maximum(block, 0) * BROWS, BROWS)
    return block >= 0, table_ref.at[pl.ds(start, BROWS)]


def run_moves(moves):
    for live, copies in moves:

        @pl.when(live)
        def _(copies=copies):
            for copy in copies:
                copy.start()

    for live, copies in moves:

        @pl.when(live)
        def _(copies=copies):
            for copy in copies:
                copy.wait()


def cross_kernel(chunks, words_ref, table_ref, out_ref, sems):
    core = lax.axis_index("basis")
    moves = []
    for i, chunk in enumerate(chunks):
        for step in range(SIDE):
            for pair, place in enumerate(chunk):
                live, source = local_block(words_ref, table_ref, reached(step, 1 - core, *place))
                at = (i, step, pair)
                moves.append((live, (pltpu.make_async_copy(source, out_ref.at[at], sems.at[at]),)))
    run_moves(moves)


def cross(chunks, words, table):
    shape = (len(chunks), SIDE, 2, BROWS, table.shape[1])
    return pl.pallas_call(
        functools.partial(cross_kernel, chunks),
        out_shape=pltpu.VMEM(shape, BF16),
        in_specs=[SMEM_SPEC, HBM_SPEC],
        out_specs=VMEM_SPEC,
        scratch_shapes=[pltpu.SemaphoreType.DMA((len(chunks), SIDE, 2))],
        compiler_params=pltpu.CompilerParams(vmem_limit_bytes=VMEM_SMALL),
        cost_estimate=SMALL,
        name="cross",
    )(words, in_hbm(table))


def pick_kernel(chunk, row, words_ref, table_ref, crossed_ref, *rest):
    outs, sems = rest[: len(HOP1)], rest[len(HOP1)]
    core = lax.axis_index("basis")
    moves = []
    for j, step in enumerate(HOP1):
        for pair, place in enumerate(chunk):
            live, source = local_block(words_ref, table_ref, reached(step, core, *place))
            copies = (
                pltpu.make_async_copy(source, outs[j].at[pair, 0], sems.at[0, j, pair]),
                pltpu.make_async_copy(crossed_ref.at[row, step, pair], outs[j].at[pair, 1], sems.at[1, j, pair]),
            )
            moves.append((live, copies))
    run_moves(moves)


def pick(chunk, row, words, table, crossed):
    return pl.pallas_call(
        functools.partial(pick_kernel, chunk, row),
        out_shape=[pltpu.VMEM((2, 2, BROWS, table.shape[1]), BF16)] * len(HOP1),
        in_specs=[SMEM_SPEC, HBM_SPEC, VMEM_SPEC],
        out_specs=[VMEM_SPEC] * len(HOP1),
        scratch_shapes=[pltpu.SemaphoreType.DMA((2, len(HOP1), 2))],
        compiler_params=pltpu.CompilerParams(vmem_limit_bytes=VMEM_SMALL),
        cost_estimate=SMALL,
        name="pick",
    )(words, in_hbm(table), in_vmem(crossed))


def project_kernel(chunk, row, added, words_ref, table_ref, own_basis, other_basis, notes_ref, coeffs_ref, crossed_ref, *rest):
    received, rest = rest[: len(HOP1)], rest[len(HOP1) :]
    extra, rest = rest[: len(added)], rest[len(added) :]
    outs, (local, total, sems) = rest[:2], rest[2:]
    x, y, z, core = coordinates()
    width = table_ref.shape[1]
    along = jnp.where(core == 0, x, y)
    pieces = []
    for which, place in enumerate(chunk):
        group = reached(0, core, *place)
        for step in HOP1 + (0,):
            line = (along - step) % SIDE
            code = word(words_ref, group, line, 0)
            rels = [word(words_ref, group, line, 1 + tile) for tile in range(2)]
            copy = None
            if step == 0:
                copy = pltpu.make_async_copy(
                    local_block(words_ref, table_ref, group)[1], local.at[which], sems.at[which]
                )
                pl.when(code >= 0)(copy.start)
            pieces.append((which, step, group, line, code, rels, copy))
    codes = [[code for which_, *_, code, _, _ in pieces if which_ == which] for which in range(2)]
    low = [functools.reduce(jnp.logical_or, [(code >= 0) & (code < DST) for code in some]) for some in codes]
    high = [functools.reduce(jnp.logical_or, [code >= DST for code in some]) for some in codes]
    main = [jnp.where(has, 0, 1) for has in low]
    both = (low[0] & high[0]) | (low[1] & high[1])

    def clear(halves):
        for which in range(2):
            total[which, halves[which]] = jnp.zeros(total.shape[2:], F32)

    other = [1 - half for half in main]
    clear(main)
    pl.when(both)(lambda: clear(other))
    lane = lax.broadcasted_iota(jnp.int32, (2, BROWS), 1)
    dest = lax.broadcasted_iota(jnp.int32, (DST, BROWS), 0)
    for which, step, group, line, code, rels, copy in pieces:

        @pl.when(code >= 0)
        def _(which=which, step=step, group=group, line=line, code=code, rels=rels, copy=copy):
            half = jnp.where(code >= DST, 1, 0)
            hit = notes_ref[group, pl.ds(line, 1), :] - half * DST == dest
            coef = [
                jnp.sum(
                    jnp.where(lane == rels[tile] % DST, coeffs_ref[rels[tile] // DST], 0.0), axis=1, keepdims=True
                )
                for tile in range(2)
            ]
            weights = jnp.where(lane < TILE, coef[0], coef[1])
            chosen = []
            for k in range(2):
                weight = jnp.where(core == 0, weights[k : k + 1], weights[1 - k : 2 - k])
                round_ = weight.astype(BF16).astype(F32)
                rest_ = jnp.where(hit, weight - round_, 0.0)
                chosen.append(jnp.concatenate([jnp.where(hit, round_, 0.0), rest_], axis=1))
            chosen = jnp.concatenate(chosen, axis=0).astype(BF16)
            for part in range(2):
                if step > 0:
                    block = received[HOP1.index(step)][which, part]
                elif part == 1:
                    block = crossed_ref[row, 0, which]
                else:
                    copy.wait()
                    block = local[which]
                sums = jnp.dot(chosen, jnp.concatenate([block, block], axis=0), preferred_element_type=F32)
                column = pl.multiple_of(jnp.where(core == part, 0, width), width)
                total[which, half, :, pl.ds(column, width)] += sums

    wide = own_basis.shape[1]
    tile = 256

    def store(halves, which, here, columns):
        if which in added:
            here += extra[added.index(which)][halves[which], :, columns].astype(F32)
        outs[which][halves[which], :, columns] = here.astype(outs[which].dtype)

    def project_half(halves):
        summed = [
            jnp.concatenate(
                [total[which, halves[which], k * DST : (k + 1) * DST, :].astype(BF16) for which in range(2)], axis=0
            )
            for k in range(2)
        ]
        for start in range(0, wide, tile):
            columns = slice(start, start + tile)
            result = jnp.dot(summed[0], own_basis[:, columns], preferred_element_type=F32)
            result += jnp.dot(summed[1], other_basis[:, columns], preferred_element_type=F32)
            for which in range(2):
                store(halves, which, result[which * DST : (which + 1) * DST], columns)

    project_half(main)

    @pl.when(both)
    def _():
        project_half(other)

    @pl.when(jnp.logical_not(both))
    def _():
        for which in range(2):
            for start in range(0, wide, tile):
                store(other, which, jnp.zeros((DST, tile), F32), slice(start, start + tile))


def project(chunk, row, added, kept, words, table, *others):
    width = table.shape[1]
    wide = 2 * width
    return pl.pallas_call(
        functools.partial(project_kernel, chunk, row, added),
        out_shape=[pltpu.VMEM((2, DST, wide), F32 if which in kept else BF16) for which in range(2)],
        in_specs=[SMEM_SPEC, HBM_SPEC] + [VMEM_SPEC] * len(others),
        out_specs=[VMEM_SPEC] * 2,
        scratch_shapes=[
            pltpu.VMEM((2, BROWS, width), BF16),
            pltpu.VMEM((2, 2, 2 * DST, 2 * width), F32),
            pltpu.SemaphoreType.DMA((2,)),
        ],
        cost_estimate=pl.CostEstimate(flops=6 * 10**9, bytes_accessed=20 * 10**6, transcendentals=0),
        compiler_params=pltpu.CompilerParams(vmem_limit_bytes=VMEM_LIMIT),
        name="project",
    )(words, in_hbm(table), *map(in_vmem, others))


def join_kernel(part_ref, relayed_ref, out_ref):
    out_ref[...] = (part_ref[...] + relayed_ref[...].astype(F32)).astype(BF16)


def join(part, relayed):
    return pl.pallas_call(
        join_kernel,
        out_shape=pltpu.VMEM(part.shape, BF16),
        in_specs=[VMEM_SPEC] * 2,
        out_specs=VMEM_SPEC,
        compiler_params=pltpu.CompilerParams(vmem_limit_bytes=VMEM_SMALL),
        cost_estimate=SMALL,
        name="join",
    )(in_vmem(part), in_vmem(relayed))


def merge_kernel(*refs):
    ins, outs = refs[:6], refs[6:]
    x, y, z, core = coordinates()
    last = jnp.where(core == 0, y, x)
    matched = (x + y + z) % 2 == core
    for send, ((step, to), (other_step, other_to)) in enumerate(zip(MATCHED, UNMATCHED)):
        which = (last + jnp.where(matched, step, other_step)) % SIDE // 2
        half = jnp.where(matched, to, other_to)
        for group in range(2):

            @pl.when(which == group)
            def _(group=group, half=half, send=send):
                result = ins[3 * group][half].astype(F32)
                for other in ins[3 * group + 1 : 3 * group + 3]:
                    result += other[half].astype(F32)
                outs[send][...] = result.astype(BF16)


def merge(parts):
    return pl.pallas_call(
        merge_kernel,
        out_shape=[pltpu.VMEM(parts[0].shape[1:], BF16)] * 4,
        in_specs=[VMEM_SPEC] * len(parts),
        out_specs=[VMEM_SPEC] * 4,
        compiler_params=pltpu.CompilerParams(vmem_limit_bytes=VMEM_LIMIT),
        cost_estimate=SMALL,
        name="merge",
    )(*map(in_vmem, parts))


def degree_kernel(dests_ref, out_ref):
    rows = dests_ref.shape[1] // 2
    mine = dests_ref[:, pl.ds(pl.multiple_of(lax.axis_index("basis") * rows, BROWS), rows)]
    hit = mine == lax.broadcasted_iota(jnp.int32, (DST, rows), 0)
    count = jnp.sum(jnp.where(hit, 1.0, 0.0), axis=1, keepdims=True)
    out_ref[...] = jnp.broadcast_to(jnp.maximum(count, 1.0), out_ref.shape)


def degrees(dests):
    return pl.pallas_call(
        degree_kernel,
        out_shape=pltpu.VMEM((DST, BROWS), F32),
        in_specs=[VMEM_SPEC],
        out_specs=VMEM_SPEC,
        compiler_params=pltpu.CompilerParams(vmem_limit_bytes=2 * VMEM_SMALL),
        cost_estimate=SMALL,
        name="degree",
    )(dests)


def table_kernel(coeffs_ref, out_ref):
    rels = coeffs_ref.shape[1]
    for i in range(out_ref.shape[0]):
        here = min(DST, rels - i * DST)
        out_ref[i, :, :here] = coeffs_ref[:, i * DST : i * DST + here]


def make_table(coeffs):
    rels = coeffs.shape[0]
    return pl.pallas_call(
        table_kernel,
        out_shape=pltpu.VMEM((-(-rels // DST), 2, DST), F32),
        in_specs=[VMEM_SPEC],
        out_specs=VMEM_SPEC,
        compiler_params=pltpu.CompilerParams(vmem_limit_bytes=2 * VMEM_SMALL),
        cost_estimate=SMALL,
        name="table",
    )(coeffs.T)


def finish_kernel(degree_ref, *refs):
    ends, out_ref = refs[:-1], refs[-1]
    degree = degree_ref[...]
    for start in range(0, out_ref.shape[1], BROWS):
        here = slice(start, start + BROWS)
        summed = ends[0][:, here].astype(F32)
        for end in ends[1:]:
            summed += end[:, here].astype(F32)
        out_ref[:, here] = (summed / degree).astype(BF16)


def finish(degree, ends):
    return pl.pallas_call(
        finish_kernel,
        out_shape=jax.ShapeDtypeStruct(ends[0].shape, BF16),
        in_specs=[VMEM_SPEC] * (1 + len(ends)),
        out_specs=VMEM_SPEC,
        compiler_params=pltpu.CompilerParams(vmem_limit_bytes=2 * VMEM_SMALL),
        cost_estimate=SMALL,
        name="finish",
    )(*map(in_vmem, (degree, *ends)))


def body(features, bases, coeffs, block_lists, block_counts, tile_rel, dest_ids):
    other_basis = lax.ppermute(bases[0], "basis", CORE_SWAP)

    sent = make_notes(block_counts, dest_ids, tile_rel, block_lists.reshape(1, CHIPS))
    notes = lax.all_to_all(sent, "shard", split_axis=0, concat_axis=0, tiled=True)
    words = notes[:, SIDE:, :WORDS].reshape(-1)
    table, degree = make_table(coeffs), degrees(dest_ids)

    words, other_basis = lax.optimization_barrier((words, other_basis))
    both = bases[0], other_basis

    first = cross(CHUNKS[:1], words, features)
    first, later = lax.optimization_barrier((first, words))
    second = cross(CHUNKS[1:], later, features)
    first = lax.ppermute(first, "basis", CORE_SWAP)
    first, second = lax.optimization_barrier((first, second))
    second = lax.ppermute(second, "basis", CORE_SWAP)
    crossed = [(0, first)] + [(i, second) for i in range(len(CHUNKS) - 1)]

    def pick_chunk(i, after):
        (row, buf), (ready, _) = crossed[i], lax.optimization_barrier((words, after))
        bufs = pick(CHUNKS[i], row, ready, features, buf)
        return lax.optimization_barrier((bufs, words))

    picked, ready = [pick_chunk(0, words)[0]], words
    bufs, ready = pick_chunk(1, picked[0])
    picked.append(bufs)
    arrived, parts = [], []
    for i, (chunk, (row, buf)) in enumerate(zip(CHUNKS, crossed)):
        came = []
        for j, step in enumerate(HOP1):
            sent = picked[i][j]
            if i > 1:
                sent, arrived[-2][j] = lax.optimization_barrier((sent, arrived[-2][j]))
            came.append(lax.ppermute(sent, AXES, hop1_pairs(step)))
        arrived.append(came)
        given = [ready, features, *both, notes, table, buf, *came]
        added = ()
        if i == FROM_ABOVE:
            added, given = (1,), given + [parts[0][1]]
        part = project(chunk, row, added, (0,) if i == FROM_BELOW else (), *given)
        if i + 2 < len(CHUNKS):
            bufs, ready = pick_chunk(i + 2, part)
            picked.append(bufs)
        if i == FROM_BELOW:
            part = [join(part[0], parts[0][0]), part[1]]
            part[0], parts[0][1] = lax.optimization_barrier((part[0], parts[0][1]))
        if i == FROM_ABOVE:
            part, parts[-1] = lax.optimization_barrier((part, parts[-1]))
        if i < len(CHUNKS) - 1:
            part = [lax.ppermute(p, AXES, hop2_pairs(step)) for p, step in zip(part, (1, 3))]
        parts.append(part)
    parts = [parts[3][0], *parts[1], parts[3][1], *parts[2]]

    merged = merge(parts)
    ends = [lax.ppermute(buf, AXES, hop3_pairs(send)) for send, buf in enumerate(merged)]
    return finish(degree, ends)


def solution(mesh):
    placed = (
        P("shard", "basis"),
        P("basis", None, None),
        P(),
        P("shard", None, None),
        P("shard", None),
        P("shard", None),
        P("shard", None),
    )
    return jax.shard_map(
        body, mesh=mesh, in_specs=placed, out_specs=P(("shard", "basis"), None), check_vma=False
    )
```

```python
import functools

import jax
import jax.numpy as jnp
from jax import lax
from jax.experimental import pallas as pl
from jax.experimental.pallas import tpu as pltpu
from jax.sharding import PartitionSpec as P

BROWS = 128
TILE = 64
DST = 128
SIDE = 4
CHIPS = SIDE**3
AXES = ("shard", "basis")
CORE_SWAP = [(0, 1), (1, 0)]
CHUNKS = (((2, 0), (2, 1)), ((1, 0), (3, 0)), ((1, 1), (3, 1)), ((0, 0), (0, 1)))
FROM_BELOW, FROM_ABOVE = 1, 2
BF16 = jnp.bfloat16
F32 = jnp.float32
SMALL = pl.CostEstimate(flops=1, bytes_accessed=1, transcendentals=0)
VMEM_SMALL = 2 * 1024 * 1024
VMEM_LIMIT = 16 * 1024 * 1024


def device_id(x, y, z, core):
    return ((z % SIDE * SIDE + y % SIDE) * SIDE + x % SIDE) * 2 + core


def pairs(target):
    found = []
    for z in range(SIDE):
        for y in range(SIDE):
            for x in range(SIDE):
                for core in range(2):
                    found.append((device_id(x, y, z, core), device_id(*target(x, y, z, core))))
    assert len({to for _, to in found}) == len(found)
    return found


def hop1_pairs(step):
    return pairs(lambda x, y, z, core: (x + step, y, z, 0) if core == 0 else (x, y + step, z, 1))


def hop2_pairs(step):
    return pairs(lambda x, y, z, core: (x, y, z + step, core))


MATCHED = ((2, 1), (2, 0), (0, 0), (0, 1))
UNMATCHED = ((1, 0), (3, 1), (1, 1), (3, 0))


def hop3_pairs(send):
    def target(x, y, z, core):
        step, half = (MATCHED if (x + y + z) % 2 == core else UNMATCHED)[send]
        return (x, y + step, z, half) if core == 0 else (x + step, y, z, half)

    return pairs(target)


def coordinates():
    chip = lax.axis_index("shard")
    return chip % SIDE, chip // SIDE % SIDE, chip // (SIDE * SIDE), lax.axis_index("basis")


def group_of(x, y, z, kind, which):
    y_end = 2 * which + (x + z) % 2
    x_end = 2 * which + (y + z + 1) % 2
    return jnp.where(kind == 0, (z * SIDE + y_end) * SIDE + x, (z * SIDE + y) * SIDE + x_end)


def in_hbm(array):
    return pltpu.with_memory_space_constraint(array, pltpu.HBM)


def in_vmem(array):
    return pltpu.with_memory_space_constraint(array, pltpu.VMEM)


SMEM_SPEC = pl.BlockSpec(memory_space=pltpu.SMEM)
HBM_SPEC = pl.BlockSpec(memory_space=pltpu.HBM)
VMEM_SPEC = pl.BlockSpec(memory_space=pltpu.VMEM)


def notes_kernel(blocks, *refs):
    given, out_ref, held, sems = refs[:4], refs[4], refs[5:9], refs[9]
    copies = [pltpu.make_async_copy(a, b, sems.at[i]) for i, (a, b) in enumerate(zip(given, held))]
    for copy in copies:
        copy.start()
    for copy in copies:
        copy.wait()
    counts_ref, dests_ref, rels_ref, lists_ref = held
    rows = CHIPS * 8
    x, y, z, _ = coordinates()
    counts = counts_ref[...]
    before = (
        lax.broadcasted_iota(jnp.int32, (CHIPS, CHIPS), 0)
        < lax.broadcasted_iota(jnp.int32, (CHIPS, CHIPS), 1)
    ).astype(F32)
    used = jnp.broadcast_to(counts.astype(F32), (8, CHIPS))
    rank = jnp.dot(used, before, preferred_element_type=F32)[:1]
    where = jnp.where(counts > 0, rank, -1.0).astype(jnp.int32)
    row = lax.broadcasted_iota(jnp.int32, (rows, 1), 0)
    slot, place = row // 8, row % 8
    line = place % SIDE
    owner = jnp.where(
        (x + y + z) % 2 == 0,
        slot // SIDE * SIDE + line,
        slot // 16 * 16 + line * SIDE + slot % SIDE,
    )

    def lookup(values, index):
        lane = lax.broadcasted_iota(jnp.int32, (rows, values.shape[1]), 1)
        return jnp.sum(jnp.where(lane == index, values, 0), axis=1, keepdims=True)

    position = lookup(where, owner)
    hit = (position == lax.broadcasted_iota(jnp.int32, (rows, blocks), 1)).astype(BF16)
    dests = jnp.concatenate([dests_ref[:, p * BROWS : (p + 1) * BROWS] for p in range(blocks)], axis=0)
    dests = jnp.dot(hit, dests.astype(BF16), preferred_element_type=F32).astype(jnp.int32)
    codes = jnp.where(position < 0, -1, dests + jnp.where(position >= blocks // 2, DST, 0))
    block = lookup(jnp.where(counts > 0, lists_ref[...], -1), slot)
    lane = lax.broadcasted_iota(jnp.int32, (rows, DST), 1)
    other = jnp.where(lane == 0, codes, block)
    for tile in range(BROWS // TILE):
        rel = lookup(rels_ref[...], position * (BROWS // TILE) + tile)
        other = jnp.where(lane == 1 + tile, rel, other)
    out_ref[...] = jnp.where(place < SIDE, codes, other)


def make_notes(*given):
    return pl.pallas_call(
        functools.partial(notes_kernel, given[1].shape[1] // BROWS),
        out_shape=jax.ShapeDtypeStruct((CHIPS * 8, DST), jnp.int32),
        in_specs=[HBM_SPEC] * 4,
        out_specs=VMEM_SPEC,
        scratch_shapes=[pltpu.VMEM(array.shape, jnp.int32) for array in given] + [pltpu.SemaphoreType.DMA((4,))],
        compiler_params=pltpu.CompilerParams(vmem_limit_bytes=VMEM_LIMIT),
        name="notes",
    )(*map(in_hbm, given)).reshape(CHIPS, 8, DST)


WORDS = 4
HOP1 = (1, 3, 2)


def word(words_ref, group, line, which):
    return words_ref[(group * SIDE + line) * WORDS + which]


def reached(step, kind, step_z, which):
    x, y, z, _ = coordinates()
    x_to = jnp.where(kind == 0, (x + step) % SIDE, x)
    y_to = jnp.where(kind == 0, y, (y + step) % SIDE)
    return group_of(x_to, y_to, (z + step_z) % SIDE, kind, which)


def local_block(words_ref, table_ref, group):
    block = word(words_ref, group, 0, WORDS - 1)
    start = pl.multiple_of(jnp.maximum(block, 0) * BROWS, BROWS)
    return block >= 0, table_ref.at[pl.ds(start, BROWS)]


def run_moves(moves):
    for live, copies in moves:

        @pl.when(live)
        def _(copies=copies):
            for copy in copies:
                copy.start()

    for live, copies in moves:

        @pl.when(live)
        def _(copies=copies):
            for copy in copies:
                copy.wait()


def cross_kernel(chunks, words_ref, table_ref, out_ref, sems):
    core = lax.axis_index("basis")
    moves = []
    for i, chunk in enumerate(chunks):
        for step in range(SIDE):
            for pair, place in enumerate(chunk):
                live, source = local_block(words_ref, table_ref, reached(step, 1 - core, *place))
                at = (i, step, pair)
                moves.append((live, (pltpu.make_async_copy(source, out_ref.at[at], sems.at[at]),)))
    run_moves(moves)


def cross(chunks, words, table):
    shape = (len(chunks), SIDE, 2, BROWS, table.shape[1])
    return pl.pallas_call(
        functools.partial(cross_kernel, chunks),
        out_shape=pltpu.VMEM(shape, BF16),
        in_specs=[SMEM_SPEC, HBM_SPEC],
        out_specs=VMEM_SPEC,
        scratch_shapes=[pltpu.SemaphoreType.DMA((len(chunks), SIDE, 2))],
        compiler_params=pltpu.CompilerParams(vmem_limit_bytes=VMEM_SMALL),
        cost_estimate=SMALL,
        name="cross",
    )(words, in_hbm(table))


def pick_kernel(chunk, row, words_ref, table_ref, crossed_ref, *rest):
    outs, sems = rest[: len(HOP1)], rest[len(HOP1)]
    core = lax.axis_index("basis")
    moves = []
    for j, step in enumerate(HOP1):
        for pair, place in enumerate(chunk):
            live, source = local_block(words_ref, table_ref, reached(step, core, *place))
            copies = (
                pltpu.make_async_copy(source, outs[j].at[pair, 0], sems.at[0, j, pair]),
                pltpu.make_async_copy(crossed_ref.at[row, step, pair], outs[j].at[pair, 1], sems.at[1, j, pair]),
            )
            moves.append((live, copies))
    run_moves(moves)


def pick(chunk, row, words, table, crossed):
    return pl.pallas_call(
        functools.partial(pick_kernel, chunk, row),
        out_shape=[pltpu.VMEM((2, 2, BROWS, table.shape[1]), BF16)] * len(HOP1),
        in_specs=[SMEM_SPEC, HBM_SPEC, VMEM_SPEC],
        out_specs=[VMEM_SPEC] * len(HOP1),
        scratch_shapes=[pltpu.SemaphoreType.DMA((2, len(HOP1), 2))],
        compiler_params=pltpu.CompilerParams(vmem_limit_bytes=VMEM_SMALL),
        cost_estimate=SMALL,
        name="pick",
    )(words, in_hbm(table), in_vmem(crossed))


def project_kernel(chunk, row, added, words_ref, table_ref, own_basis, other_basis, notes_ref, coeffs_ref, crossed_ref, *rest):
    received, rest = rest[: len(HOP1)], rest[len(HOP1) :]
    extra, rest = rest[: len(added)], rest[len(added) :]
    outs, (local, total, sems) = rest[:2], rest[2:]
    x, y, z, core = coordinates()
    width = table_ref.shape[1]
    along = jnp.where(core == 0, x, y)
    pieces = []
    for which, place in enumerate(chunk):
        group = reached(0, core, *place)
        for step in HOP1 + (0,):
            line = (along - step) % SIDE
            code = word(words_ref, group, line, 0)
            rels = [word(words_ref, group, line, 1 + tile) for tile in range(2)]
            copy = None
            if step == 0:
                copy = pltpu.make_async_copy(
                    local_block(words_ref, table_ref, group)[1], local.at[which], sems.at[which]
                )
                pl.when(code >= 0)(copy.start)
            pieces.append((which, step, group, line, code, rels, copy))
    codes = [[code for which_, *_, code, _, _ in pieces if which_ == which] for which in range(2)]
    low = [functools.reduce(jnp.logical_or, [(code >= 0) & (code < DST) for code in some]) for some in codes]
    high = [functools.reduce(jnp.logical_or, [code >= DST for code in some]) for some in codes]
    main = [jnp.where(has, 0, 1) for has in low]
    both = (low[0] & high[0]) | (low[1] & high[1])

    def clear(halves):
        for which in range(2):
            total[which, halves[which]] = jnp.zeros(total.shape[2:], F32)

    other = [1 - half for half in main]
    clear(main)
    pl.when(both)(lambda: clear(other))
    lane = lax.broadcasted_iota(jnp.int32, (2, BROWS), 1)
    dest = lax.broadcasted_iota(jnp.int32, (DST, BROWS), 0)
    for which, step, group, line, code, rels, copy in pieces:

        @pl.when(code >= 0)
        def _(which=which, step=step, group=group, line=line, code=code, rels=rels, copy=copy):
            half = jnp.where(code >= DST, 1, 0)
            hit = notes_ref[group, pl.ds(line, 1), :] - half * DST == dest
            coef = [
                jnp.sum(
                    jnp.where(lane == rels[tile] % DST, coeffs_ref[rels[tile] // DST], 0.0), axis=1, keepdims=True
                )
                for tile in range(2)
            ]
            weights = jnp.where(lane < TILE, coef[0], coef[1])
            chosen = []
            for k in range(2):
                weight = jnp.where(core == 0, weights[k : k + 1], weights[1 - k : 2 - k])
                round_ = weight.astype(BF16).astype(F32)
                rest_ = jnp.where(hit, weight - round_, 0.0)
                chosen.append(jnp.concatenate([jnp.where(hit, round_, 0.0), rest_], axis=1))
            chosen = jnp.concatenate(chosen, axis=0).astype(BF16)
            for part in range(2):
                if step > 0:
                    block = received[HOP1.index(step)][which, part]
                elif part == 1:
                    block = crossed_ref[row, 0, which]
                else:
                    copy.wait()
                    block = local[which]
                sums = jnp.dot(chosen, jnp.concatenate([block, block], axis=0), preferred_element_type=F32)
                column = pl.multiple_of(jnp.where(core == part, 0, width), width)
                total[which, half, :, pl.ds(column, width)] += sums

    wide = own_basis.shape[1]
    tile = 512

    def store(halves, which, here, columns):
        if which in added:
            here += extra[added.index(which)][halves[which], :, columns].astype(F32)
        outs[which][halves[which], :, columns] = here.astype(outs[which].dtype)

    def project_half(halves):
        summed = [
            jnp.concatenate(
                [total[which, halves[which], k * DST : (k + 1) * DST, :].astype(BF16) for which in range(2)], axis=0
            )
            for k in range(2)
        ]
        for start in range(0, wide, tile):
            columns = slice(start, start + tile)
            result = jnp.dot(summed[0], own_basis[:, columns], preferred_element_type=F32)
            result += jnp.dot(summed[1], other_basis[:, columns], preferred_element_type=F32)
            for which in range(2):
                store(halves, which, result[which * DST : (which + 1) * DST], columns)

    project_half(main)

    @pl.when(both)
    def _():
        project_half(other)

    @pl.when(jnp.logical_not(both))
    def _():
        for which in range(2):
            for start in range(0, wide, tile):
                store(other, which, jnp.zeros((DST, tile), F32), slice(start, start + tile))


def project(chunk, row, added, kept, words, table, *others):
    width = table.shape[1]
    wide = 2 * width
    return pl.pallas_call(
        functools.partial(project_kernel, chunk, row, added),
        out_shape=[pltpu.VMEM((2, DST, wide), F32 if which in kept else BF16) for which in range(2)],
        in_specs=[SMEM_SPEC, HBM_SPEC] + [VMEM_SPEC] * len(others),
        out_specs=[VMEM_SPEC] * 2,
        scratch_shapes=[
            pltpu.VMEM((2, BROWS, width), BF16),
            pltpu.VMEM((2, 2, 2 * DST, 2 * width), F32),
            pltpu.SemaphoreType.DMA((2,)),
        ],
        cost_estimate=pl.CostEstimate(flops=6 * 10**9, bytes_accessed=20 * 10**6, transcendentals=0),
        compiler_params=pltpu.CompilerParams(vmem_limit_bytes=VMEM_LIMIT),
        name="project",
    )(words, in_hbm(table), *map(in_vmem, others))


def join_kernel(part_ref, relayed_ref, out_ref):
    out_ref[...] = (part_ref[...] + relayed_ref[...].astype(F32)).astype(BF16)


def join(part, relayed):
    return pl.pallas_call(
        join_kernel,
        out_shape=pltpu.VMEM(part.shape, BF16),
        in_specs=[VMEM_SPEC] * 2,
        out_specs=VMEM_SPEC,
        compiler_params=pltpu.CompilerParams(vmem_limit_bytes=VMEM_SMALL),
        cost_estimate=SMALL,
        name="join",
    )(in_vmem(part), in_vmem(relayed))


def merge_kernel(*refs):
    ins, outs = refs[:6], refs[6:]
    x, y, z, core = coordinates()
    last = jnp.where(core == 0, y, x)
    matched = (x + y + z) % 2 == core
    for send, ((step, to), (other_step, other_to)) in enumerate(zip(MATCHED, UNMATCHED)):
        which = (last + jnp.where(matched, step, other_step)) % SIDE // 2
        half = jnp.where(matched, to, other_to)
        for group in range(2):

            @pl.when(which == group)
            def _(group=group, half=half, send=send):
                result = ins[3 * group][half].astype(F32)
                for other in ins[3 * group + 1 : 3 * group + 3]:
                    result += other[half].astype(F32)
                outs[send][...] = result.astype(BF16)


def merge(parts):
    return pl.pallas_call(
        merge_kernel,
        out_shape=[pltpu.VMEM(parts[0].shape[1:], BF16)] * 4,
        in_specs=[VMEM_SPEC] * len(parts),
        out_specs=[VMEM_SPEC] * 4,
        compiler_params=pltpu.CompilerParams(vmem_limit_bytes=VMEM_LIMIT),
        cost_estimate=SMALL,
        name="merge",
    )(*map(in_vmem, parts))


def degree_kernel(dests_ref, out_ref):
    rows = dests_ref.shape[1] // 2
    mine = dests_ref[:, pl.ds(pl.multiple_of(lax.axis_index("basis") * rows, BROWS), rows)]
    hit = mine == lax.broadcasted_iota(jnp.int32, (DST, rows), 0)
    count = jnp.sum(jnp.where(hit, 1.0, 0.0), axis=1, keepdims=True)
    out_ref[...] = jnp.broadcast_to(jnp.maximum(count, 1.0), out_ref.shape)


def degrees(dests):
    return pl.pallas_call(
        degree_kernel,
        out_shape=pltpu.VMEM((DST, BROWS), F32),
        in_specs=[VMEM_SPEC],
        out_specs=VMEM_SPEC,
        compiler_params=pltpu.CompilerParams(vmem_limit_bytes=2 * VMEM_SMALL),
        cost_estimate=SMALL,
        name="degree",
    )(dests)


def table_kernel(coeffs_ref, out_ref):
    rels = coeffs_ref.shape[1]
    for i in range(out_ref.shape[0]):
        here = min(DST, rels - i * DST)
        out_ref[i, :, :here] = coeffs_ref[:, i * DST : i * DST + here]


def make_table(coeffs):
    rels = coeffs.shape[0]
    return pl.pallas_call(
        table_kernel,
        out_shape=pltpu.VMEM((-(-rels // DST), 2, DST), F32),
        in_specs=[VMEM_SPEC],
        out_specs=VMEM_SPEC,
        compiler_params=pltpu.CompilerParams(vmem_limit_bytes=2 * VMEM_SMALL),
        cost_estimate=SMALL,
        name="table",
    )(coeffs.T)


def finish_kernel(degree_ref, *refs):
    ends, out_ref = refs[:-1], refs[-1]
    degree = degree_ref[...]
    for start in range(0, out_ref.shape[1], BROWS):
        here = slice(start, start + BROWS)
        summed = ends[0][:, here].astype(F32)
        for end in ends[1:]:
            summed += end[:, here].astype(F32)
        out_ref[:, here] = (summed / degree).astype(BF16)


def finish(degree, ends):
    return pl.pallas_call(
        finish_kernel,
        out_shape=jax.ShapeDtypeStruct(ends[0].shape, BF16),
        in_specs=[VMEM_SPEC] * (1 + len(ends)),
        out_specs=VMEM_SPEC,
        compiler_params=pltpu.CompilerParams(vmem_limit_bytes=2 * VMEM_SMALL),
        cost_estimate=SMALL,
        name="finish",
    )(*map(in_vmem, (degree, *ends)))


def body(features, bases, coeffs, block_lists, block_counts, tile_rel, dest_ids):
    other_basis = lax.ppermute(bases[0], "basis", CORE_SWAP)

    sent = make_notes(block_counts, dest_ids, tile_rel, block_lists.reshape(1, CHIPS))
    notes = lax.all_to_all(sent, "shard", split_axis=0, concat_axis=0, tiled=True)
    words = notes[:, SIDE:, :WORDS].reshape(-1)
    table, degree = make_table(coeffs), degrees(dest_ids)

    words, other_basis = lax.optimization_barrier((words, other_basis))
    both = bases[0], other_basis

    first = cross(CHUNKS[:1], words, features)
    first, later = lax.optimization_barrier((first, words))
    second = cross(CHUNKS[1:], later, features)
    first = lax.ppermute(first, "basis", CORE_SWAP)
    first, second = lax.optimization_barrier((first, second))
    second = lax.ppermute(second, "basis", CORE_SWAP)
    crossed = [(0, first)] + [(i, second) for i in range(len(CHUNKS) - 1)]

    def pick_chunk(i, after):
        (row, buf), (ready, _) = crossed[i], lax.optimization_barrier((words, after))
        bufs = pick(CHUNKS[i], row, ready, features, buf)
        return lax.optimization_barrier((bufs, words))

    picked, ready = [pick_chunk(0, words)[0]], words
    bufs, ready = pick_chunk(1, picked[0])
    picked.append(bufs)
    arrived, parts = [], []
    for i, (chunk, (row, buf)) in enumerate(zip(CHUNKS, crossed)):
        came = []
        for j, step in enumerate(HOP1):
            sent = picked[i][j]
            if i > 1:
                sent, arrived[-2][j] = lax.optimization_barrier((sent, arrived[-2][j]))
            came.append(lax.ppermute(sent, AXES, hop1_pairs(step)))
        arrived.append(came)
        given = [ready, features, *both, notes, table, buf, *came]
        added = ()
        if i == FROM_ABOVE:
            added, given = (1,), given + [parts[0][1]]
        part = project(chunk, row, added, (0,) if i == FROM_BELOW else (), *given)
        if i + 2 < len(CHUNKS):
            bufs, ready = pick_chunk(i + 2, part)
            picked.append(bufs)
        if i == FROM_BELOW:
            part = [join(part[0], parts[0][0]), part[1]]
            part[0], parts[0][1] = lax.optimization_barrier((part[0], parts[0][1]))
        if i == FROM_ABOVE:
            part, parts[-1] = lax.optimization_barrier((part, parts[-1]))
        if i < len(CHUNKS) - 1:
            part = [lax.ppermute(p, AXES, hop2_pairs(step)) for p, step in zip(part, (1, 3))]
        parts.append(part)
    parts = [parts[3][0], *parts[1], parts[3][1], *parts[2]]

    merged = merge(parts)
    ends = [lax.ppermute(buf, AXES, hop3_pairs(send)) for send, buf in enumerate(merged)]
    return finish(degree, ends)


def solution(mesh):
    placed = (
        P("shard", "basis"),
        P("basis", None, None),
        P(),
        P("shard", None, None),
        P("shard", None),
        P("shard", None),
        P("shard", None),
    )
    return jax.shard_map(
        body, mesh=mesh, in_specs=placed, out_specs=P(("shard", "basis"), None), check_vma=False
    )
```
